256 devices in a mesh: span: 4 (over z_hi, core), tok: 64 (over y, z_lo, x).
Axes of the slice: x: 4, y: 4, z: 8 (z_hi: 2, z_lo: 4; z = z_hi * 4 + z_lo), core: 2. Of those that a mesh axis runs over, the one named last changes fastest.
Arguments:
- latent: float32 [4, 2048, 64], P('span', 'tok'), may hold values from -6 to 6
- step_index: int32 [4], replicated, may hold values from 0 to 6
- w_query: bfloat16 [64, 4096], replicated, as said below
- w_key: bfloat16 [64, 4096], replicated, as said below
- w_value: bfloat16 [64, 4096], replicated, may hold values from -0.75 to 0.75
- cond: float32 [3, 4096], replicated, may hold values from -3 to 3
- qk_gain: float32 [2, 32], replicated, may hold values from 0.8 to 6, as said below
- w_out: bfloat16 [4096, 64], replicated, may hold values from -0.09375 to 0.09375
Outputs:
- latent_out: float32 [4, 2048, 64], P('span', 'tok')
- velocity: float32 [4, 2048, 64], P('span', 'tok')
The draws below stay inside these ranges and needn't reach their ends.
Inputs may be any that keep to these rules, and one draw needn't show every extreme that they name: `w_query`: query projection, fan-in scaled. `w_key`: key projection, fan-in scaled. `qk_gain`: positive gains.
All inputs are finite; a program needn't handle non-finite values.
Results may differ from the reference program's by a relative error of at most 0.008.
Values may be sent and summed in bfloat16 or wider, within the bound.
A program may use at most 64 MiB of HBM per device.

```python
import jax
import jax.numpy as jnp
from jax import lax

P_SIZE = 64
HEADS = 32
HEAD_DIM = 128
NSTEPS = 8
WIDTH = 4096
NCH = 4
SEQ = 2048
N_SPAN = 4


def common_matrix(key):
    return jax.random.normal(key, (P_SIZE, WIDTH), jnp.float32)


def draw_w_query(key, part):
    shared = common_matrix(key)
    return (shared * P_SIZE ** (-0.5)).astype(jnp.bfloat16)


def draw_w_key(key, part):
    key = jax.random.fold_in(key, 2)
    own = jax.random.normal(key, (P_SIZE, WIDTH), jnp.float32)
    mixed = own
    return (mixed * P_SIZE ** (-0.5)).astype(jnp.bfloat16)


def draw_qk_gain(key, part):
    key = jax.random.fold_in(key, 3)
    unit = jax.random.uniform(key, (2, HEADS), jnp.float32)
    low, high = (0.8, 3.0)
    return jnp.exp(jnp.log(low) + unit * (jnp.log(high) - jnp.log(low)))


def plant(values, key, smallest, top_value):
    extent = values.shape
    index_at = [jax.random.randint(jax.random.fold_in(key, axis), (), 0, extent[axis]) for axis in range(len(extent))]
    values = values.at[tuple(index_at)].set(smallest)
    longest = extent.index(max(extent))
    index_at[longest] = (index_at[longest] + 1) % extent[longest]
    return values.at[tuple(index_at)].set(top_value)


def level_of(rng, dims, shards, least, top_value):
    factor_of = 1.0
    for axis_at, shards_of in shards:
        draws = jax.random.uniform(jax.random.fold_in(jax.random.fold_in(rng, 6), axis_at), (shards_of,), jnp.float32, least / len(shards), top_value / len(shards))
        factor_of = factor_of * jnp.repeat(jnp.exp(draws), dims[axis_at] // shards_of).reshape((-1,) + (1,) * (len(dims) - 1 - axis_at))
    return factor_of


def scatter_about(own_key, dims, scale, limit, shards=(), kind=jnp.bfloat16):
    result = jax.random.normal(own_key, dims, jnp.float32) * scale
    if len(shards) > 0:
        result = level_of(own_key, dims, shards, -0.22, 0.18) * result
    return jnp.clip(result, min=-limit, max=limit).astype(kind)


def setup_inputs(seed: int = 0) -> dict:
    seeds = jax.random.split(jax.random.key(seed), 9)
    latent = scatter_about(seeds[0], (NCH, SEQ, P_SIZE), 1.0, 6.0, ((0, 4), (1, 64)), jnp.float32)
    step_index = plant(jax.random.randint(seeds[1], (NCH,), 0, NSTEPS - 1), jax.random.fold_in(seeds[1], 1), 0, (NSTEPS - 1) - 1).astype(jnp.int32)
    w_query = draw_w_query(jax.random.fold_in(seeds[8], 71), 0)
    w_key = draw_w_key(jax.random.fold_in(seeds[8], 71), 0)
    w_value = scatter_about(seeds[4], (P_SIZE, WIDTH), P_SIZE ** -0.5, 0.75)
    cond = scatter_about(seeds[5], (3, WIDTH), 0.5, 3.0, (), jnp.float32)
    qk_gain = draw_qk_gain(jax.random.fold_in(seeds[8], 71), 0)
    w_out = scatter_about(seeds[7], (WIDTH, P_SIZE), WIDTH ** -0.5, 0.09375)
    return {"latent": latent, "step_index": step_index, "w_query": w_query, "w_key": w_key, "w_value": w_value, "cond": cond, "qk_gain": qk_gain, "w_out": w_out}


def sigma_at(level):
    frac = 1.0 - level / NSTEPS
    return 3.0 * frac / (1.0 + 2.0 * frac)

def block_terms(queries, keys, values):
    scores = jnp.dot(queries, keys.T, preferred_element_type=jnp.float32) * HEAD_DIM ** (-0.5)
    top = lax.optimization_barrier(jnp.max(scores, axis=-1))
    expo = jnp.exp(scores - top[:, None])
    total = lax.optimization_barrier(jnp.sum(expo, axis=-1))
    acc = jnp.dot(expo.astype(jnp.bfloat16), values, preferred_element_type=jnp.float32)
    return (top, acc, total)

def one_head(packed):
    queries, keys, values = packed
    outs = []
    for span in range(N_SPAN):
        terms = [block_terms(queries[span], keys[other], values[other]) for other in range(span + 1)]
        biggest = terms[0][0]
        for item in terms[1:]:
            biggest = jnp.maximum(biggest, item[0])
        acc = jnp.zeros((SEQ, HEAD_DIM), jnp.float32)
        total = jnp.zeros((SEQ,), jnp.float32)
        for item in terms:
            factor = jnp.exp(item[0] - biggest)
            acc = acc + factor[:, None] * item[1]
            total = total + factor * item[2]
        outs.append(acc / total[:, None])
    return jnp.stack(outs)

def reference(latent, step_index, w_query, w_key, w_value, cond, qk_gain, w_out):
    state = latent
    levels = step_index.astype(jnp.float32)
    velocity = jnp.zeros_like(latent)
    for step in range(2):
        sig = sigma_at(levels + step)
        sig_next = sigma_at(levels + step + 1)
        flat = state.reshape(N_SPAN * SEQ, P_SIZE).astype(jnp.bfloat16)
        shift = jnp.repeat(sig, SEQ)[:, None]

        def project(weight, row):
            return jnp.dot(flat, weight, preferred_element_type=jnp.float32) + shift * cond[row][None, :]

        def normed(value, row):
            split = value.reshape(N_SPAN * SEQ, HEADS, HEAD_DIM)
            rms = jnp.sqrt(lax.optimization_barrier(jnp.mean(split * split, axis=-1, keepdims=True)) + 1e-06)
            return (split / rms * qk_gain[row][None, :, None]).astype(jnp.bfloat16)
        query = normed(project(w_query, 0), 0)
        key_all = normed(project(w_key, 1), 1)
        value_all = project(w_value, 2).astype(jnp.bfloat16).reshape(N_SPAN * SEQ, HEADS, HEAD_DIM)

        def heads_first(array):
            return array.reshape(N_SPAN, SEQ, HEADS, HEAD_DIM).transpose(2, 0, 1, 3)
        attended = lax.map(one_head, (heads_first(query), heads_first(key_all), heads_first(value_all)))
        attended = attended.astype(jnp.bfloat16).transpose(1, 2, 0, 3).reshape(N_SPAN * SEQ, WIDTH)
        velocity = jnp.dot(attended, w_out, preferred_element_type=jnp.float32).reshape(N_SPAN, SEQ, P_SIZE)
        state = state + (sig_next - sig)[:, None, None] * velocity
    return (state, velocity)
```

```python
import functools

import jax
import jax.numpy as jnp
from jax import lax
from jax.experimental import pallas as pl
from jax.experimental.pallas import tpu as pltpu
from jax.sharding import PartitionSpec as P

MESH = pl.DeviceIdType.MESH
NSTEPS = 8
ROWS = 32
CHANS = 64
HEADS = 32
HD = 128
WIDTH = HEADS * HD
SEQ = 2048
PIECE = 4 * ROWS
CHUNK = 16 * ROWS
TILE_HEADS = 8
TILE = TILE_HEADS * ROWS
LOG2E = 1.4426950408889634
BF = jnp.bfloat16
F32 = jnp.float32


def dot_nt(a, b):
    return lax.dot_general(a, b, (((1,), (1,)), ((), ())), preferred_element_type=F32)


def dot_nn(a, b):
    return jnp.dot(a, b, preferred_element_type=F32)


def kernel(
    step_ref, gain_ref, latent_ref, cond_ref, wq_hbm, wk_hbm, wv_hbm, wo_hbm,
    state_out, vel_out,
    grid, wq, wk, wv, wo, aug, state, q2, acc, top, rsc, att,
    wsem, zs, zr, p2s, p2r, p3s, p3r, cs, cr,
):
    c = lax.axis_index("span")
    t = lax.axis_index("tok")
    hi = c // 2
    core = c % 2
    y = t // 16
    zl = (t // 4) % 4
    x = t % 4

    def tok(yy, zz, xx):
        return yy * 16 + zz * 4 + xx

    loads = [
        pltpu.make_async_copy(wk_hbm, wk.at[pl.ds(0, CHANS), :], wsem.at[0]),
        pltpu.make_async_copy(wq_hbm, wq.at[pl.ds(0, CHANS), :], wsem.at[1]),
        pltpu.make_async_copy(wv_hbm, wv.at[pl.ds(0, CHANS), :], wsem.at[2]),
        pltpu.make_async_copy(wo_hbm, wo, wsem.at[3]),
    ]
    for item in loads:
        item.start()

    barrier = pltpu.get_barrier_semaphore()

    def greet(span, token):
        pl.semaphore_signal(barrier, inc=1, device_id=(span, token), device_id_type=MESH)

    other = (1 - hi) * 2 + core
    for d in range(1, 4):
        greet(c, tok(y, (zl + d) % 4, x))
        greet(c, tok((y + d) % 4, zl, x))
        greet(c, tok(y, zl, (x + d) % 4))
    for d in range(4):
        greet(other, tok(y, d, x))
    greet(hi * 2 + 1 - core, t)

    lane = lax.broadcasted_iota(jnp.int32, (1, 128), 1)
    row16 = lax.broadcasted_iota(jnp.int32, (16, WIDTH), 0)
    for which, ref in enumerate((wq, wk, wv)):
        cvec = cond_ref[which : which + 1, :]
        chi = cvec.astype(BF).astype(F32)
        clo = cvec - chi
        rows = jnp.where((row16 == 0) | (row16 == 2), chi, jnp.where(row16 == 1, clo, 0.0))
        ref[CHANS : CHANS + 16, :] = rows.astype(BF)
        ref[CHANS + 16 :, :] = jnp.zeros((128 - CHANS - 16, WIDTH), BF)
    gk = jnp.zeros((1, 128), F32)
    for h in range(HEADS):
        gk = jnp.where((lane == CHANS + h) | (lane == CHANS + HEADS + h), gain_ref[1, h], gk)
    gk = gk * (HD ** (-0.5) * LOG2E)
    selr = lax.broadcasted_iota(jnp.int32, (HEADS, 128), 0)
    sell = lax.broadcasted_iota(jnp.int32, (HEADS, 128), 1)
    sel = jnp.where((sell == CHANS + selr) | (sell == CHANS + HEADS + selr), 1.0, 0.0).astype(BF)
    pmask = jnp.where(lane < CHANS, 1.0, 0.0)
    state[...] = jnp.zeros_like(state)
    state[:, 0:CHANS] = latent_ref[...]

    def sigma(span, extra):
        level = jnp.full((1, 128), step_ref[span] + extra, jnp.int32).astype(F32)
        frac = 1.0 - level / NSTEPS
        return 3.0 * frac / (1.0 + 2.0 * frac)

    pl.semaphore_wait(barrier, 14)
    loads[0].wait()

    def rail(r, kk):
        along_x = kk == r
        return along_x, jnp.where(along_x, x, y), jnp.where(along_x, y, x)

    def inner_tok(along_x, i):
        return jnp.where(along_x, tok(y, zl, i), tok(i, zl, x))

    def outer_tok(along_x, o):
        return jnp.where(along_x, tok(o, zl, x), tok(y, zl, o))

    def rdma(ref, send, recv, dev):
        return pltpu.make_async_remote_copy(
            src_ref=ref, dst_ref=ref, send_sem=send, recv_sem=recv, device_id=dev, device_id_type=MESH
        )

    def step(s, carry):
        for span in range(4):
            sig = sigma(span, s)
            shi = sig.astype(BF).astype(F32)
            slo = sig - shi
            row = jnp.where(
                (lane == CHANS) | (lane == CHANS + 1),
                shi,
                jnp.where(lane == CHANS + 2, slo, jnp.where(lane == CHANS + 3, 1.0, 0.0)),
            )
            aug[span] = jnp.broadcast_to(row, (8, 128))
        patches = state[...]
        own = (patches + aug[c][0:1, :]).astype(BF)

        squares = jnp.zeros((ROWS, 128), F32)
        for h in range(HEADS):
            pk = dot_nn(own, wk[:, h * HD : (h + 1) * HD])
            ms = jnp.sum(pk * pk, axis=-1, keepdims=True)
            squares = jnp.where((lane == CHANS + h) | (lane == CHANS + HEADS + h), ms, squares)
        factor = gk / jnp.sqrt(squares * (1.0 / HD) + 1e-06)
        fhi = factor.astype(BF).astype(F32)
        row = jnp.where(lane < CHANS, patches, jnp.where(lane < CHANS + HEADS, fhi, factor - fhi))
        _, inner0, outer0 = rail(hi, core)
        first = (outer0 * 16 + inner0 * 4 + zl) * ROWS
        grid[s, c, pl.ds(pl.multiple_of(first, ROWS), ROWS), :] = row.astype(BF)

        def zblock(e, zz):
            r = e // 2
            _, i, o = rail(r, e % 2)
            at = pl.multiple_of((o * 16 + i * 4 + zz) * ROWS, ROWS)
            return grid.at[s, e, pl.ds(at, ROWS), :]

        def piece(e, o, i):
            at = pl.multiple_of((o * 4 + i) * PIECE, PIECE)
            return grid.at[s, e, pl.ds(at, PIECE), :]

        def chunk_of(e, o):
            at = pl.multiple_of(o * CHUNK, CHUNK)
            return grid.at[s, e, pl.ds(at, CHUNK), :]

        def z_copy(d):
            return rdma(zblock(c, zl), zs.at[s, d - 1], zr.at[s, hi, zl], (c, tok(y, (zl + d) % 4, x)))

        def up_copy(d):
            return rdma(zblock(c, zl), zs.at[s, 3 + d], zr.at[s, 0, zl], (other, tok(y, d, x)))

        def z_wait(r, zz):
            e = core + 2 * r
            rdma(zblock(e, zz), zs.at[s, 0], zr.at[s, r, zz], (c, t)).wait_recv()

        for d in range(1, 4):
            z_copy(d).start()

        @pl.when(hi == 0)
        def _():
            for d in range(4):
                up_copy(d).start()

        def p2_copy(r, d):
            e = core + 2 * r
            along_x, i, o = rail(r, core)
            return rdma(piece(e, o, i), p2s.at[s, r, d - 1], p2r.at[s, r, i], (c, inner_tok(along_x, (i + d) % 4)))

        def p3_copy(r, i, d):
            e = core + 2 * r
            along_x, _, o = rail(r, core)
            return rdma(
                piece(e, o, i), p3s.at[s, r, i, d - 1], p3r.at[s, r, o, i], (c, outer_tok(along_x, (o + d) % 4))
            )

        def core_copy(r, o):
            e = core + 2 * r
            return rdma(chunk_of(e, o), cs.at[s, r, o], cr.at[s, r, o], (hi * 2 + 1 - core, t))

        @pl.when(s == 0)
        def _():
            loads[1].wait()

        for h in range(HEADS):
            pq = dot_nn(own, wq[:, h * HD : (h + 1) * HD])
            ms = jnp.sum(pq * pq, axis=-1, keepdims=True) * (1.0 / HD)
            qn = (pq / jnp.sqrt(ms + 1e-06) * gain_ref[0, h]).astype(BF)
            qk = dot_nt(qn, wk[:, h * HD : (h + 1) * HD])
            qhi = qk.astype(BF)
            q2[h * ROWS : (h + 1) * ROWS, 0:128] = qhi
            q2[h * ROWS : (h + 1) * ROWS, 128:256] = (qk - qhi.astype(F32)).astype(BF)
        acc[...] = jnp.zeros_like(acc)
        top[...] = jnp.full_like(top, -1e30)

        def second(r, carry):
            @pl.when(r == hi)
            def _():
                for d in range(1, 4):
                    z_wait(r, (zl + d) % 4)

            @pl.when(r != hi)
            def _():
                for d in range(4):
                    z_wait(r, d)

            _, i, _ = rail(r, core)
            for d in range(1, 4):
                p2_copy(r, d).start()
            for d in range(1, 4):
                p3_copy(r, i, d).start()
            return carry

        lax.fori_loop(0, hi + 1, second, 0)

        def third(r, carry):
            e = core + 2 * r
            _, i, o = rail(r, core)
            for d in range(1, 4):
                ii = (i + d) % 4
                rdma(piece(e, o, ii), p2s.at[s, r, 0], p2r.at[s, r, ii], (c, t)).wait_recv()
                for dd in range(1, 4):
                    p3_copy(r, ii, dd).start()
            return carry

        lax.fori_loop(0, hi + 1, third, 0)

        def attend(e, o):
            g = chunk_of(e, o)[...]
            g2 = (g * pmask.astype(BF) + aug[e][0:1, :].astype(BF))
            keys = jnp.concatenate([g2, g2], axis=1)
            rsc[...] = dot_nt(sel, g)
            for tile in range(HEADS // TILE_HEADS):
                base = tile * TILE
                scores = dot_nt(q2[base : base + TILE, :], keys)
                parts = []
                for k in range(TILE_HEADS):
                    h = tile * TILE_HEADS + k
                    at = slice(h * ROWS, (h + 1) * ROWS)
                    sh = scores[k * ROWS : (k + 1) * ROWS, :] * rsc[h : h + 1, :]
                    old = top[at, :]
                    new = jnp.maximum(old, jnp.max(sh, axis=-1, keepdims=True))
                    top[at, :] = new
                    acc[at, :] = acc[at, :] * jnp.exp2(old - new)
                    parts.append(jnp.exp2(sh - new[:, 0:1]).astype(BF))
                acc[base : base + TILE, :] += dot_nn(jnp.concatenate(parts, axis=0), g2)

        def outer_loop(k, carry):
            off = k ^ (k // 2)

            def inner_loop(j, carry):
                mine = j <= hi
                e = jnp.where(mine, c - 2 * j, c - 1 - 2 * (j - hi - 1))
                r = e // 2
                _, _, o = rail(r, e % 2)
                b = (o + off) % 4

                @pl.when(mine)
                def _():
                    @pl.when(k > 0)
                    def _():
                        for i in range(4):
                            rdma(piece(e, b, i), p3s.at[s, r, 0, 0], p3r.at[s, r, b, i], (c, t)).wait_recv()

                    @pl.when(r <= hi - core)
                    def _():
                        core_copy(r, b).start()

                @pl.when(jnp.logical_not(mine))
                def _():
                    rdma(chunk_of(e, b), cs.at[s, 0, 0], cr.at[s, r, b], (c, t)).wait_recv()

                attend(e, b)
                return carry

            lax.fori_loop(0, c + 1, inner_loop, 0)
            return carry

        lax.fori_loop(0, 4, outer_loop, 0)

        @pl.when(s == 0)
        def _():
            loads[2].wait()
            loads[3].wait()

        for h in range(HEADS):
            a = acc[h * ROWS : (h + 1) * ROWS, :]
            z = a / a[:, CHANS + 3 : CHANS + 4]
            zhi = z.astype(BF)
            zlo = (z - zhi.astype(F32)).astype(BF)
            both = dot_nn(jnp.concatenate([zhi, zlo], axis=0), wv[:, h * HD : (h + 1) * HD])
            att[:, h * HD : (h + 1) * HD] = (both[0:ROWS] + both[ROWS:]).astype(BF)
        velocity = dot_nn(att[...], wo[...])
        change = sigma(c, s + 1) - sigma(c, s)
        state[:, 0:CHANS] = state[:, 0:CHANS] + change[:, 0:CHANS] * velocity
        vel_out[...] = velocity

        for d in range(1, 4):
            z_copy(d).wait_send()

        @pl.when(hi == 0)
        def _():
            for d in range(4):
                up_copy(d).wait_send()

        def drain(r, carry):
            for d in range(1, 4):
                p2_copy(r, d).wait_send()
            for i in range(4):
                for d in range(1, 4):
                    p3_copy(r, i, d).wait_send()

            @pl.when(r <= hi - core)
            def _():
                for o in range(4):
                    core_copy(r, o).wait_send()

            return carry

        lax.fori_loop(0, hi + 1, drain, 0)
        return carry

    lax.fori_loop(0, 2, step, 0)
    state_out[...] = state[:, 0:CHANS]


def local(latent, step_index, w_query, w_key, w_value, cond, qk_gain, w_out):
    vmem = pl.BlockSpec(memory_space=pltpu.VMEM)
    smem = pl.BlockSpec(memory_space=pltpu.SMEM)
    hbm = pl.BlockSpec(memory_space=pl.ANY)
    dma = pltpu.SemaphoreType.DMA
    out = jax.ShapeDtypeStruct((ROWS, CHANS), F32)
    state, velocity = pl.pallas_call(
        kernel,
        out_shape=(out, out),
        in_specs=[smem, smem, vmem, vmem, hbm, hbm, hbm, hbm],
        out_specs=(vmem, vmem),
        scratch_shapes=[
            pltpu.VMEM((2, 4, SEQ, 128), BF),
            pltpu.VMEM((128, WIDTH), BF),
            pltpu.VMEM((128, WIDTH), BF),
            pltpu.VMEM((128, WIDTH), BF),
            pltpu.VMEM((WIDTH, CHANS), BF),
            pltpu.VMEM((4, 8, 128), F32),
            pltpu.VMEM((ROWS, 128), F32),
            pltpu.VMEM((HEADS * ROWS, 256), BF),
            pltpu.VMEM((HEADS * ROWS, 128), F32),
            pltpu.VMEM((HEADS * ROWS, 128), F32),
            pltpu.VMEM((HEADS, CHUNK), F32),
            pltpu.VMEM((ROWS, WIDTH), BF),
            dma((4,)),
            dma((2, 7)),
            dma((2, 2, 4)),
            dma((2, 2, 3)),
            dma((2, 2, 4)),
            dma((2, 2, 4, 3)),
            dma((2, 2, 4, 4)),
            dma((2, 2, 4)),
            dma((2, 2, 4)),
        ],
        compiler_params=pltpu.CompilerParams(
            collective_id=0, has_side_effects=True, vmem_limit_bytes=48 * 1024 * 1024
        ),
    )(step_index, qk_gain, latent[0], cond, w_query, w_key, w_value, w_out)
    return state[None], velocity[None]


def solution(mesh):
    return jax.shard_map(
        local,
        mesh=mesh,
        in_specs=(P("span", "tok", None), P(), P(), P(), P(), P(), P(), P()),
        out_specs=(P("span", "tok", None), P("span", "tok", None)),
        check_vma=False,
    )
```

```python
import functools

import jax
import jax.numpy as jnp
from jax import lax
from jax.experimental import pallas as pl
from jax.experimental.pallas import tpu as pltpu
from jax.sharding import PartitionSpec as P

MESH = pl.DeviceIdType.MESH
NSTEPS = 8
ROWS = 32
CHANS = 64
HEADS = 32
HD = 128
WIDTH = HEADS * HD
SEQ = 2048
PIECE = 4 * ROWS
CHUNK = 16 * ROWS
QUERIES = HEADS * ROWS
COLS = QUERIES // 2
GROUP = 4
SUB = 64
LOG2E = 1.4426950408889634
BF = jnp.bfloat16
F32 = jnp.float32


def dot_nt(a, b):
    return lax.dot_general(a, b, (((1,), (1,)), ((), ())), preferred_element_type=F32)


def dot_nn(a, b):
    return jnp.dot(a, b, preferred_element_type=F32)


def kernel(
    step_ref, gain_ref, latent_ref, cond_ref, wq_hbm, wk_hbm, wv_hbm, wo_hbm,
    state_out, vel_out,
    grid, wq, wk, wv, wo, aug, state, q2, flat, acc, top,
    wsem, zs, zr, p2s, p2r, p3s, p3r, cs, cr,
):
    c = lax.axis_index("span")
    t = lax.axis_index("tok")
    hi = c // 2
    core = c % 2
    y = t // 16
    zl = (t // 4) % 4
    x = t % 4

    def tok(yy, zz, xx):
        return yy * 16 + zz * 4 + xx

    loads = [
        pltpu.make_async_copy(wk_hbm, wk.at[pl.ds(0, CHANS), :], wsem.at[0]),
        pltpu.make_async_copy(wq_hbm, wq.at[pl.ds(0, CHANS), :], wsem.at[1]),
        pltpu.make_async_copy(wv_hbm, wv.at[pl.ds(0, CHANS), :], wsem.at[2]),
        pltpu.make_async_copy(wo_hbm, wo, wsem.at[3]),
    ]
    for item in loads:
        item.start()

    barrier = pltpu.get_barrier_semaphore()

    def greet(span, token):
        pl.semaphore_signal(barrier, inc=1, device_id=(span, token), device_id_type=MESH)

    other = (1 - hi) * 2 + core
    for d in range(1, 4):
        greet(c, tok(y, (zl + d) % 4, x))
        greet(c, tok((y + d) % 4, zl, x))
        greet(c, tok(y, zl, (x + d) % 4))
    for d in range(4):
        greet(other, tok(y, d, x))
    greet(hi * 2 + 1 - core, t)

    lane = lax.broadcasted_iota(jnp.int32, (1, 128), 1)
    row16 = lax.broadcasted_iota(jnp.int32, (16, WIDTH), 0)
    for which, ref in enumerate((wq, wk, wv)):
        cvec = cond_ref[which : which + 1, :]
        chi = cvec.astype(BF).astype(F32)
        clo = cvec - chi
        rows = jnp.where((row16 == 0) | (row16 == 2), chi, jnp.where(row16 == 1, clo, 0.0))
        ref[CHANS : CHANS + 16, :] = rows.astype(BF)
        ref[CHANS + 16 :, :] = jnp.zeros((128 - CHANS - 16, WIDTH), BF)
    gk = jnp.zeros((1, 128), F32)
    for h in range(HEADS):
        gk = jnp.where((lane == CHANS + h) | (lane == CHANS + HEADS + h), gain_ref[1, h], gk)
    gk = gk * (HD ** (-0.5) * LOG2E)
    down = lax.broadcasted_iota(jnp.int32, (128, 128), 0)
    across = lax.broadcasted_iota(jnp.int32, (128, 128), 1)
    spread = jnp.where((down >= CHANS) & (down % HEADS == across % HEADS), 1.0, 0.0).astype(BF)
    eye = jnp.where(down == across, 1.0, 0.0).astype(BF)
    pmask = jnp.where(lane < CHANS, 1.0, 0.0)
    state[...] = jnp.zeros_like(state)
    state[:, 0:CHANS] = latent_ref[...]

    def sigma(span, extra):
        level = jnp.full((1, 128), step_ref[span] + extra, jnp.int32).astype(F32)
        frac = 1.0 - level / NSTEPS
        return 3.0 * frac / (1.0 + 2.0 * frac)

    pl.semaphore_wait(barrier, 14)
    loads[0].wait()

    def rail(r, kk):
        along_x = kk == r
        return along_x, jnp.where(along_x, x, y), jnp.where(along_x, y, x)

    def inner_tok(along_x, i):
        return jnp.where(along_x, tok(y, zl, i), tok(i, zl, x))

    def outer_tok(along_x, o):
        return jnp.where(along_x, tok(o, zl, x), tok(y, zl, o))

    def rdma(ref, send, recv, dev):
        return pltpu.make_async_remote_copy(
            src_ref=ref, dst_ref=ref, send_sem=send, recv_sem=recv, device_id=dev, device_id_type=MESH
        )

    def step(s, carry):
        for span in range(4):
            sig = sigma(span, s)
            shi = sig.astype(BF).astype(F32)
            slo = sig - shi
            row = jnp.where(
                (lane == CHANS) | (lane == CHANS + 1),
                shi,
                jnp.where(lane == CHANS + 2, slo, jnp.where(lane == CHANS + 3, 1.0, 0.0)),
            )
            aug[span] = jnp.broadcast_to(row, (8, 128))
        patches = state[...]
        own = (patches + aug[c][0:1, :]).astype(BF)

        squares = jnp.zeros((ROWS, 128), F32)
        pk = dot_nn(own, wk[...])
        for h in range(HEADS):
            part = pk[:, h * HD : (h + 1) * HD]
            ms = jnp.sum(part * part, axis=-1, keepdims=True)
            squares = jnp.where((lane == CHANS + h) | (lane == CHANS + HEADS + h), ms, squares)
        factor = gk / jnp.sqrt(squares * (1.0 / HD) + 1e-06)
        fhi = factor.astype(BF).astype(F32)
        row = jnp.where(lane < CHANS, patches, jnp.where(lane < CHANS + HEADS, fhi, factor - fhi))
        _, inner0, outer0 = rail(hi, core)
        first = (outer0 * 16 + inner0 * 4 + zl) * ROWS
        grid[s, c, pl.ds(pl.multiple_of(first, ROWS), ROWS), :] = row.astype(BF)

        def zblock(e, zz):
            r = e // 2
            _, i, o = rail(r, e % 2)
            at = pl.multiple_of((o * 16 + i * 4 + zz) * ROWS, ROWS)
            return grid.at[s, e, pl.ds(at, ROWS), :]

        def piece(e, o, i):
            at = pl.multiple_of((o * 4 + i) * PIECE, PIECE)
            return grid.at[s, e, pl.ds(at, PIECE), :]

        def chunk_of(e, o):
            at = pl.multiple_of(o * CHUNK, CHUNK)
            return grid.at[s, e, pl.ds(at, CHUNK), :]

        def z_copy(d):
            return rdma(zblock(c, zl), zs.at[s, d - 1], zr.at[s, hi, zl], (c, tok(y, (zl + d) % 4, x)))

        def up_copy(d):
            return rdma(zblock(c, zl), zs.at[s, 3 + d], zr.at[s, 0, zl], (other, tok(y, d, x)))

        def z_wait(r, zz):
            e = core + 2 * r
            rdma(zblock(e, zz), zs.at[s, 0], zr.at[s, r, zz], (c, t)).wait_recv()

        for d in range(1, 4):
            z_copy(d).start()

        @pl.when(hi == 0)
        def _():
            for d in range(4):
                up_copy(d).start()

        def p2_copy(r, d):
            e = core + 2 * r
            along_x, i, o = rail(r, core)
            return rdma(piece(e, o, i), p2s.at[s, r, d - 1], p2r.at[s, r, i], (c, inner_tok(along_x, (i + d) % 4)))

        def p3_copy(r, i, d):
            e = core + 2 * r
            along_x, _, o = rail(r, core)
            return rdma(
                piece(e, o, i), p3s.at[s, r, i, d - 1], p3r.at[s, r, o, i], (c, outer_tok(along_x, (o + d) % 4))
            )

        def core_copy(r, o):
            e = core + 2 * r
            return rdma(chunk_of(e, o), cs.at[s, r, o], cr.at[s, r, o], (hi * 2 + 1 - core, t))

        @pl.when(s == 0)
        def _():
            loads[1].wait()

        pq = dot_nn(own, wq[...])
        normed = []
        for h in range(HEADS):
            part = pq[:, h * HD : (h + 1) * HD]
            ms = jnp.sum(part * part, axis=-1, keepdims=True) * (1.0 / HD)
            normed.append((part / jnp.sqrt(ms + 1e-06) * gain_ref[0, h]).astype(BF))
        for h in range(HEADS):
            flat[pl.ds(h, ROWS, stride=HEADS), :] = dot_nt(normed[h], wk[:, h * HD : (h + 1) * HD])
        qk = flat[...]
        qhi = qk.astype(BF)
        q2[:, 0:128] = qhi
        q2[:, 128:256] = (qk - qhi.astype(F32)).astype(BF)
        acc[...] = jnp.zeros_like(acc)
        top[...] = jnp.full_like(top, -1e30)

        def second(r, carry):
            @pl.when(r == hi)
            def _():
                for d in range(1, 4):
                    z_wait(r, (zl + d) % 4)

            @pl.when(r != hi)
            def _():
                for d in range(4):
                    z_wait(r, d)

            _, i, _ = rail(r, core)
            for d in range(1, 4):
                p2_copy(r, d).start()
            for d in range(1, 4):
                p3_copy(r, i, d).start()
            return carry

        lax.fori_loop(0, hi + 1, second, 0)

        def third(r, carry):
            e = core + 2 * r
            _, i, o = rail(r, core)
            for d in range(1, 4):
                ii = (i + d) % 4
                rdma(piece(e, o, ii), p2s.at[s, r, 0], p2r.at[s, r, ii], (c, t)).wait_recv()
                for dd in range(1, 4):
                    p3_copy(r, ii, dd).start()
            return carry

        lax.fori_loop(0, hi + 1, third, 0)

        def attend(blocks):
            keys, factors, turned = [], [], []
            for e, o in blocks:
                g = chunk_of(e, o)[...]
                g2 = g * pmask.astype(BF) + aug[e][0:1, :].astype(BF)
                keys.append(jnp.concatenate([g2, g2], axis=1))
                factors.append(dot_nn(g, spread))
                turned.append(dot_nt(eye, g2).astype(BF))
            units = [(k, u) for k in range(len(blocks)) for u in range(QUERIES // COLS)]

            def score(n):
                k, u = units[n]
                return dot_nt(keys[k], q2[u * COLS : (u + 1) * COLS, :])

            def soften(n, raw):
                k, u = units[n]
                cols = slice(u * COLS, (u + 1) * COLS)
                scaled, best = [], None
                for at in range(0, CHUNK, SUB):
                    wide = jnp.concatenate([factors[k][at : at + SUB, :]] * (COLS // 128), axis=1)
                    part = raw[at : at + SUB, :] * wide
                    scaled.append(part)
                    high = jnp.max(part.reshape(SUB // 8, 8, COLS), axis=0)
                    best = high if best is None else jnp.maximum(best, high)
                old = top[0:1, cols]
                new = jnp.maximum(old, jnp.max(best, axis=0, keepdims=True))
                top[0:1, cols] = new
                weights = [jnp.exp2(part - new).astype(BF) for part in scaled]
                return n, jnp.concatenate(weights, axis=0), jnp.exp2(old - new)

            def gather(n, weights, alpha):
                k, u = units[n]
                cols = slice(u * COLS, (u + 1) * COLS)
                acc[:, cols] = acc[:, cols] * alpha + dot_nn(turned[k], weights)

            raw = score(0)
            pending = None
            for n in range(len(units)):
                later = score(n + 1) if n + 1 < len(units) else None
                ready = soften(n, raw)
                if pending is not None:
                    gather(*pending)
                pending, raw = ready, later
            gather(*pending)

        def place(n):
            k, j = n // (c + 1), n % (c + 1)
            mine = j <= hi
            e = jnp.where(mine, c - 2 * j, c - 1 - 2 * (j - hi - 1))
            _, _, o = rail(e // 2, e % 2)
            return k, mine, e, e // 2, (o + (k ^ (k // 2))) % 4

        def group(m, carry):
            def arrive(q, carry):
                k, mine, e, r, b = place(GROUP * m + q)

                @pl.when(mine)
                def _():
                    @pl.when(k > 0)
                    def _():
                        for i in range(4):
                            rdma(piece(e, b, i), p3s.at[s, r, 0, 0], p3r.at[s, r, b, i], (c, t)).wait_recv()

                    @pl.when(r <= hi - core)
                    def _():
                        core_copy(r, b).start()

                return carry

            def cross(q, carry):
                k, mine, e, r, b = place(GROUP * m + q)

                @pl.when(jnp.logical_not(mine))
                def _():
                    rdma(chunk_of(e, b), cs.at[s, 0, 0], cr.at[s, r, b], (c, t)).wait_recv()

                return carry

            lax.fori_loop(0, GROUP, arrive, 0)
            lax.fori_loop(0, GROUP, cross, 0)
            blocks = []
            for q in range(GROUP):
                _, _, e, _, b = place(GROUP * m + q)
                blocks.append((e, b))
            attend(blocks)
            return carry

        lax.fori_loop(0, c + 1, group, 0)

        @pl.when(s == 0)
        def _():
            loads[2].wait()
            loads[3].wait()

        sums = acc[...]
        flat[...] = (sums / sums[CHANS + 3 : CHANS + 4, :]).T
        attended = []
        for h in range(HEADS):
            z = flat[pl.ds(h, ROWS, stride=HEADS), :]
            zhi = z.astype(BF)
            zlo = (z - zhi.astype(F32)).astype(BF)
            both = dot_nn(jnp.concatenate([zhi, zlo], axis=0), wv[:, h * HD : (h + 1) * HD])
            attended.append((both[0:ROWS] + both[ROWS:]).astype(BF))
        velocity = dot_nt(jnp.concatenate(attended, axis=1), wo[...])
        change = sigma(c, s + 1) - sigma(c, s)
        state[:, 0:CHANS] = state[:, 0:CHANS] + change[:, 0:CHANS] * velocity
        vel_out[...] = velocity

        for d in range(1, 4):
            z_copy(d).wait_send()

        @pl.when(hi == 0)
        def _():
            for d in range(4):
                up_copy(d).wait_send()

        def drain(r, carry):
            for d in range(1, 4):
                p2_copy(r, d).wait_send()
            for i in range(4):
                for d in range(1, 4):
                    p3_copy(r, i, d).wait_send()

            @pl.when(r <= hi - core)
            def _():
                for o in range(4):
                    core_copy(r, o).wait_send()

            return carry

        lax.fori_loop(0, hi + 1, drain, 0)
        return carry

    lax.fori_loop(0, 2, step, 0)
    state_out[...] = state[:, 0:CHANS]


def local(latent, step_index, w_query, w_key, w_value, cond, qk_gain, w_out):
    vmem = pl.BlockSpec(memory_space=pltpu.VMEM)
    smem = pl.BlockSpec(memory_space=pltpu.SMEM)
    hbm = pl.BlockSpec(memory_space=pl.ANY)
    dma = pltpu.SemaphoreType.DMA
    out = jax.ShapeDtypeStruct((ROWS, CHANS), F32)
    state, velocity = pl.pallas_call(
        kernel,
        out_shape=(out, out),
        in_specs=[smem, smem, vmem, vmem, hbm, hbm, hbm, hbm],
        out_specs=(vmem, vmem),
        scratch_shapes=[
            pltpu.VMEM((2, 4, SEQ, 128), BF),
            pltpu.VMEM((128, WIDTH), BF),
            pltpu.VMEM((128, WIDTH), BF),
            pltpu.VMEM((128, WIDTH), BF),
            pltpu.VMEM((CHANS, WIDTH), BF),
            pltpu.VMEM((4, 8, 128), F32),
            pltpu.VMEM((ROWS, 128), F32),
            pltpu.VMEM((QUERIES, 256), BF),
            pltpu.VMEM((QUERIES, 128), F32),
            pltpu.VMEM((128, QUERIES), F32),
            pltpu.VMEM((8, QUERIES), F32),
            dma((4,)),
            dma((2, 7)),
            dma((2, 2, 4)),
            dma((2, 2, 3)),
            dma((2, 2, 4)),
            dma((2, 2, 4, 3)),
            dma((2, 2, 4, 4)),
            dma((2, 2, 4)),
            dma((2, 2, 4)),
        ],
        compiler_params=pltpu.CompilerParams(
            collective_id=0, has_side_effects=True, vmem_limit_bytes=48 * 1024 * 1024
        ),
    )(step_index, qk_gain, latent[0], cond, w_query, w_key, w_value, w_out.T)
    return state[None], velocity[None]


def solution(mesh):
    return jax.shard_map(
        local,
        mesh=mesh,
        in_specs=(P("span", "tok", None), P(), P(), P(), P(), P(), P(), P()),
        out_specs=(P("span", "tok", None), P("span", "tok", None)),
        check_vma=False,
    )
```

```python
import jax
import jax.numpy as jnp
from jax import lax
from jax.experimental import pallas as pl
from jax.experimental.pallas import tpu as pltpu
from jax.sharding import PartitionSpec as P

MESH = pl.DeviceIdType.MESH
NSTEPS = 8
ROWS = 32
HALF = 16
CHANS = 64
HEADS = 32
HD = 128
WIDTH = HEADS * HD
SEQ = 2048
CHUNK = SEQ // 4
QUERIES = HEADS * ROWS
COLS = QUERIES // 2
SUB = 64
LAG = 2
LOG2E = 1.4426950408889634
BF = jnp.bfloat16
F32 = jnp.float32


def dot_nt(a, b):
    return lax.dot_general(a, b, (((1,), (1,)), ((), ())), preferred_element_type=F32)


def dot_nn(a, b):
    return jnp.dot(a, b, preferred_element_type=F32)


def kernel(
    step_ref, gain_ref, latent_ref, cond_ref, wq_hbm, wk_hbm, wv_hbm, wo_hbm,
    state_out, vel_out,
    grid, wq, wk, wv, wo, aug, state, swap, result, back, q2, flat, acc, top, accx, topx,
    wsem, zs, zr, p2s, p2r, p3s, p3r, cs, cr, xs, xr,
):
    c = lax.axis_index("span")
    t = lax.axis_index("tok")
    zhi = c // 2
    core = c % 2
    kind = jnp.where(zhi == core, 0, 1)
    y = t // 16
    zl = (t // 4) % 4
    x = t % 4
    z = zhi * 4 + zl
    along_x = kind == 0
    inner = jnp.where(along_x, x, y)
    outer = jnp.where(along_x, y, x)

    def tok(yy, zz, xx):
        return yy * 16 + zz * 4 + xx

    def z_peer(d):
        zz = (z + d) % 8
        up = zz // 4
        return kind + up * (3 - 2 * kind), tok(y, zz % 4, x)

    def inner_peer(d):
        i = (inner + d) % 4
        return c, jnp.where(along_x, tok(y, zl, i), tok(i, zl, x))

    def outer_peer(d):
        o = (outer + d) % 4
        return c, jnp.where(along_x, tok(o, zl, x), tok(y, zl, o))

    mate = (zhi * 2 + 1 - core, t)

    loads = [
        pltpu.make_async_copy(wk_hbm, wk.at[pl.ds(0, CHANS), :], wsem.at[0]),
        pltpu.make_async_copy(wq_hbm, wq.at[pl.ds(0, CHANS), :], wsem.at[1]),
        pltpu.make_async_copy(wv_hbm, wv.at[pl.ds(0, CHANS), :], wsem.at[2]),
        pltpu.make_async_copy(wo_hbm, wo, wsem.at[3]),
    ]
    for item in loads:
        item.start()

    barrier = pltpu.get_barrier_semaphore()

    def greet(dev):
        pl.semaphore_signal(barrier, inc=1, device_id=dev, device_id_type=MESH)

    for d in range(1, 8):
        greet(z_peer(d))
    for d in range(1, 4):
        greet(inner_peer(d))
        greet(outer_peer(d))
    greet(mate)

    lane = lax.broadcasted_iota(jnp.int32, (1, 128), 1)
    low = lax.broadcasted_iota(jnp.int32, (ROWS, 128), 0) < HALF
    row16 = lax.broadcasted_iota(jnp.int32, (16, WIDTH), 0)
    for which, ref in enumerate((wq, wk, wv)):
        cvec = cond_ref[which : which + 1, :]
        chi = cvec.astype(BF).astype(F32)
        clo = cvec - chi
        rows = jnp.where((row16 == 0) | (row16 == 2), chi, jnp.where(row16 == 1, clo, 0.0))
        ref[CHANS : CHANS + 16, :] = rows.astype(BF)
        ref[CHANS + 16 :, :] = jnp.zeros((128 - CHANS - 16, WIDTH), BF)
    gk = jnp.zeros((1, 128), F32)
    for h in range(HEADS):
        gk = jnp.where((lane == CHANS + h) | (lane == CHANS + HEADS + h), gain_ref[1, h], gk)
    gk = gk * (HD ** (-0.5) * LOG2E)
    down = lax.broadcasted_iota(jnp.int32, (128, 128), 0)
    across = lax.broadcasted_iota(jnp.int32, (128, 128), 1)
    spread = jnp.where((down >= CHANS) & (down % HEADS == across % HEADS), 1.0, 0.0).astype(BF)
    eye = jnp.where(down == across, 1.0, 0.0).astype(BF)
    pmask = jnp.where(lane < CHANS, 1.0, 0.0)
    state[...] = jnp.zeros_like(state)

    def sigma(span, extra):
        level = jnp.full((1, 128), step_ref[span] + extra, jnp.int32).astype(F32)
        frac = 1.0 - level / NSTEPS
        return 3.0 * frac / (1.0 + 2.0 * frac)

    def rdma(src, dst, send, recv, dev):
        return pltpu.make_async_remote_copy(
            src_ref=src, dst_ref=dst, send_sem=send, recv_sem=recv, device_id=dev, device_id_type=MESH
        )

    def drain(ref, sem):
        pltpu.make_async_copy(ref, ref, sem).wait()

    def half_of(n):
        return pl.ds(pl.multiple_of(n * HALF, HALF), HALF)

    pl.semaphore_wait(barrier, 14)
    give = rdma(latent_ref.at[half_of(1 - zhi), :], swap.at[half_of(zhi), :], xs.at[0], xr.at[0], z_peer(4))
    give.start()
    give.wait_recv()
    mine = (lax.broadcasted_iota(jnp.int32, (ROWS, CHANS), 0) < HALF) == (zhi == 0)
    state[:, 0:CHANS] = jnp.where(mine, latent_ref[...], swap[...])
    loads[0].wait()

    def step(s, carry):
        def area(which, blk, count):
            at = pl.multiple_of(blk * HALF, HALF)
            return grid.at[s, which, :, pl.ds(at, count * HALF), :]

        def chunk_of(which, half, o):
            at = pl.multiple_of(o * CHUNK, CHUNK)
            return grid.at[s, which, half, pl.ds(at, CHUNK), :]

        augs = []
        for span in range(4):
            sig = sigma(span, s)
            shi = sig.astype(BF).astype(F32)
            slo = sig - shi
            augs.append(
                jnp.where(
                    (lane == CHANS) | (lane == CHANS + 1),
                    shi,
                    jnp.where(lane == CHANS + 2, slo, jnp.where(lane == CHANS + 3, 1.0, 0.0)),
                )
            )
            aug[span] = jnp.broadcast_to(augs[span], (8, 128))
        patches = state[...]
        own = (patches + jnp.where(low, aug[kind][0:1, :], aug[3 - kind][0:1, :])).astype(BF)

        squares = jnp.zeros((ROWS, 128), F32)
        pk = dot_nn(own, wk[...])
        for h in range(HEADS):
            part = pk[:, h * HD : (h + 1) * HD]
            ms = jnp.sum(part * part, axis=-1, keepdims=True)
            squares = jnp.where((lane == CHANS + h) | (lane == CHANS + HEADS + h), ms, squares)
        factor = gk / jnp.sqrt(squares * (1.0 / HD) + 1e-06)
        fhi = factor.astype(BF).astype(F32)
        row = jnp.where(lane < CHANS, patches, jnp.where(lane < CHANS + HEADS, fhi, factor - fhi)).astype(BF)
        blk = outer * 32 + inner * 8 + z
        mine_at = pl.ds(pl.multiple_of(blk * HALF, HALF), HALF)
        grid[s, kind, 0, mine_at, :] = row[0:HALF]
        grid[s, kind, 1, mine_at, :] = row[HALF:]

        block = area(kind, blk, 1)
        for d in range(1, 8):
            rdma(block, block, zs.at[s], zr.at[s], z_peer(d)).start()

        @pl.when(s == 0)
        def _():
            loads[1].wait()

        pq = dot_nn(own, wq[...])
        normed = []
        for h in range(HEADS):
            part = pq[:, h * HD : (h + 1) * HD]
            ms = jnp.sum(part * part, axis=-1, keepdims=True) * (1.0 / HD)
            normed.append((part / jnp.sqrt(ms + 1e-06) * gain_ref[0, h]).astype(BF))
        for h in range(HEADS):
            flat[pl.ds(h, ROWS, stride=HEADS), :] = dot_nt(normed[h], wk[:, h * HD : (h + 1) * HD])

        drain(area(kind, 0, 7), zr.at[s])
        line = area(kind, outer * 32 + inner * 8, 8)
        for d in range(1, 4):
            rdma(line, line, p2s.at[s], p2r.at[s], inner_peer(d)).start()

        qk = flat[...]
        qhi = qk.astype(BF)
        q2[:, 0:128] = qhi
        q2[:, 128:256] = (qk - qhi.astype(F32)).astype(BF)
        for ref in (acc, accx):
            ref[...] = jnp.zeros_like(ref)
        for ref in (top, topx):
            ref[...] = jnp.full_like(ref, -1e30)

        drain(area(kind, 0, 24), p2r.at[s])
        plane = area(kind, outer * 32, 32)
        for d in (1, 3, 2):
            rdma(plane, plane, p3s.at[s], p3r.at[s, outer], outer_peer(d)).start()

        def share(k):
            @pl.when(kind == 0)
            def _():
                ref = chunk_of(0, 0, (y + k) % 4)
                rdma(ref, ref, cs.at[s], cr.at[s, k], mate).start()

            @pl.when(kind == 1)
            def _():
                ref = area(1, ((x + k) % 4) * 32, 32)
                rdma(ref, ref, cs.at[s], cr.at[s, k], mate).start()

        def shared(k):
            @pl.when(kind == 0)
            def _():
                drain(area(1, 0, 32), cr.at[s, k])

            @pl.when(kind == 1)
            def _():
                drain(chunk_of(0, 0, 0), cr.at[s, k])

        def arrived(k):
            drain(area(kind, 0, 32), p3r.at[s, (outer + k) % 4])

        def attend(k):
            at_a, at_b = (y + k) % 4, (x + k) % 4
            blocks = [
                (0, chunk_of(0, 0, at_a)),
                (1, chunk_of(1, 0, at_b)),
                (2, chunk_of(1, 1, at_b)),
                (3 - 2 * kind, chunk_of(kind, 1 - kind, jnp.where(along_x, at_a, at_b))),
            ]
            keys, factors, turned = [], [], []
            for span, ref in blocks:
                g = ref[...]
                g2 = g * pmask.astype(BF) + aug[span][0:1, :].astype(BF)
                keys.append(jnp.concatenate([g2, g2], axis=1))
                factors.append(dot_nn(g, spread))
                turned.append(dot_nt(eye, g2).astype(BF))
            spare = pl.ds(pl.multiple_of((1 - kind) * COLS, COLS), COLS)
            first, second, whole = slice(0, COLS), slice(COLS, QUERIES), slice(0, COLS)
            units = [
                (0, first, top, acc, first),
                (0, second, top, acc, second),
                (3, spare, topx, accx, whole),
                (1, second, top, acc, second),
                (2, second, top, acc, second),
            ]

            def score(n):
                b, rows = units[n][:2]
                return dot_nt(keys[b], q2[rows, :])

            def soften(n, raw):
                b, _, tref, _, cols = units[n]
                scaled, best = [], None
                for at in range(0, CHUNK, SUB):
                    wide = jnp.concatenate([factors[b][at : at + SUB, :]] * (COLS // 128), axis=1)
                    part = raw[at : at + SUB, :] * wide
                    scaled.append(part)
                    high = jnp.max(part.reshape(SUB // 8, 8, COLS), axis=0)
                    best = high if best is None else jnp.maximum(best, high)
                old = tref[0:1, cols]
                new = jnp.maximum(old, jnp.max(best, axis=0, keepdims=True))
                tref[0:1, cols] = new
                weights = [jnp.exp2(part - new).astype(BF) for part in scaled]
                return n, jnp.concatenate(weights, axis=0), jnp.exp2(old - new)

            def gather(n, weights, alpha):
                b, _, _, aref, cols = units[n]
                aref[:, cols] = aref[:, cols] * alpha + dot_nn(turned[b], weights)

            raw = score(0)
            pending = []
            for n in range(len(units)):
                later = score(n + 1) if n + 1 < len(units) else None
                pending.append(soften(n, raw))
                raw = later
                if len(pending) > LAG:
                    gather(*pending.pop(0))
            for item in pending:
                gather(*item)

        share(0)
        shared(0)

        def group(m, carry):
            attend(m ^ (m // 2))

            @pl.when(m == 0)
            def _():
                arrived(1)
                share(1)
                arrived(3)
                share(3)
                shared(1)

            @pl.when(m == 1)
            def _():
                shared(3)

            @pl.when(m == 2)
            def _():
                arrived(2)
                share(2)
                shared(2)

            return carry

        lax.fori_loop(0, 4, group, 0)

        @pl.when(s == 0)
        def _():
            loads[2].wait()
            loads[3].wait()

        joined = []
        for u in range(2):
            cols = slice(u * COLS, (u + 1) * COLS)
            there = kind == 1 - u
            extra = jnp.where(there, topx[0:1, :], -1e30)
            new = jnp.maximum(top[0:1, cols], extra)
            joined.append(
                acc[:, cols] * jnp.exp2(top[0:1, cols] - new)
                + accx[...] * jnp.where(there, jnp.exp2(extra - new), 0.0)
            )
        sums = jnp.concatenate(joined, axis=1)
        flat[...] = (sums / sums[CHANS + 3 : CHANS + 4, :]).T
        attended = []
        for h in range(HEADS):
            zed = flat[pl.ds(h, ROWS, stride=HEADS), :]
            zed_hi = zed.astype(BF)
            zed_lo = (zed - zed_hi.astype(F32)).astype(BF)
            both = dot_nn(jnp.concatenate([zed_hi, zed_lo], axis=0), wv[:, h * HD : (h + 1) * HD])
            attended.append((both[0:ROWS] + both[ROWS:]).astype(BF))
        velocity = dot_nt(jnp.concatenate(attended, axis=1), wo[...])
        lo_change = sigma(kind, s + 1) - sigma(kind, s)
        hi_change = sigma(3 - kind, s + 1) - sigma(3 - kind, s)
        change = jnp.where(low, lo_change, hi_change)
        state[:, 0:CHANS] = state[:, 0:CHANS] + change[:, 0:CHANS] * velocity
        result[1] = velocity

        drain(area(kind, 0, 7), zs.at[s])
        drain(area(kind, 0, 24), p2s.at[s])
        drain(area(kind, 0, 96), p3s.at[s])

        @pl.when(kind == 0)
        def _():
            drain(grid.at[s, 0, 0], cs.at[s])

        @pl.when(kind == 1)
        def _():
            drain(grid.at[s, 1], cs.at[s])

        return carry

    lax.fori_loop(0, 2, step, 0)
    result[0] = state[:, 0:CHANS]
    give_back = rdma(result.at[:, half_of(1 - zhi), :], back.at[:, half_of(zhi), :], xs.at[1], xr.at[1], z_peer(4))
    give_back.start()
    give_back.wait_recv()
    state_out[...] = jnp.where(mine, result[0], back[0])
    vel_out[...] = jnp.where(mine, result[1], back[1])
    give.wait_send()
    give_back.wait_send()


def local(latent, step_index, w_query, w_key, w_value, cond, qk_gain, w_out):
    vmem = pl.BlockSpec(memory_space=pltpu.VMEM)
    smem = pl.BlockSpec(memory_space=pltpu.SMEM)
    hbm = pl.BlockSpec(memory_space=pl.ANY)
    dma = pltpu.SemaphoreType.DMA
    out = jax.ShapeDtypeStruct((ROWS, CHANS), F32)
    state, velocity = pl.pallas_call(
        kernel,
        out_shape=(out, out),
        in_specs=[smem, smem, vmem, vmem, hbm, hbm, hbm, hbm],
        out_specs=(vmem, vmem),
        scratch_shapes=[
            pltpu.VMEM((2, 2, 2, SEQ, 128), BF),
            pltpu.VMEM((128, WIDTH), BF),
            pltpu.VMEM((128, WIDTH), BF),
            pltpu.VMEM((128, WIDTH), BF),
            pltpu.VMEM((CHANS, WIDTH), BF),
            pltpu.VMEM((4, 8, 128), F32),
            pltpu.VMEM((ROWS, 128), F32),
            pltpu.VMEM((ROWS, CHANS), F32),
            pltpu.VMEM((2, ROWS, CHANS), F32),
            pltpu.VMEM((2, ROWS, CHANS), F32),
            pltpu.VMEM((QUERIES, 256), BF),
            pltpu.VMEM((QUERIES, 128), F32),
            pltpu.VMEM((128, QUERIES), F32),
            pltpu.VMEM((8, QUERIES), F32),
            pltpu.VMEM((128, COLS), F32),
            pltpu.VMEM((8, COLS), F32),
            dma((4,)),
            dma((2,)),
            dma((2,)),
            dma((2,)),
            dma((2,)),
            dma((2,)),
            dma((2, 4)),
            dma((2,)),
            dma((2, 4)),
            dma((2,)),
            dma((2,)),
        ],
        compiler_params=pltpu.CompilerParams(
            collective_id=0, has_side_effects=True, vmem_limit_bytes=63 * 1024 * 1024
        ),
    )(step_index, qk_gain, latent[0], cond, w_query, w_key, w_value, w_out.T)
    return state[None], velocity[None]


def solution(mesh):
    return jax.shard_map(
        local,
        mesh=mesh,
        in_specs=(P("span", "tok", None), P(), P(), P(), P(), P(), P(), P()),
        out_specs=(P("span", "tok", None), P("span", "tok", None)),
        check_vma=False,
    )
```

```python
import jax
import jax.numpy as jnp
from jax import lax
from jax.experimental import pallas as pl
from jax.experimental.pallas import tpu as pltpu
from jax.sharding import PartitionSpec as P

MESH = pl.DeviceIdType.MESH
NSTEPS = 8
ROWS = 32
PIECE = 4 * ROWS
CHANS = 64
HEADS = 32
HD = 128
WIDTH = HEADS * HD
SEQ = 2048
CHUNK = SEQ // 4
QUERIES = HEADS * ROWS
COLS = QUERIES // 2
SUB = 64
LAG = 2
PLACES = (
    (0, 0), (1, 0), (3, 0), (0, 1), (0, 3), (1, 1), (3, 3), (1, 3),
    (3, 1), (2, 0), (0, 2), (2, 1), (2, 3), (1, 2), (3, 2), (2, 2),
)
SLOT = {place: n for n, place in enumerate(PLACES)}
LOG2E = 1.4426950408889634
BF = jnp.bfloat16
F32 = jnp.float32


def dot_nt(a, b):
    return lax.dot_general(a, b, (((1,), (1,)), ((), ())), preferred_element_type=F32)


def dot_nn(a, b):
    return jnp.dot(a, b, preferred_element_type=F32)


def kernel(
    step_ref, gain_ref, latent_ref, cond_ref, wq_hbm, wk_hbm, wv_hbm, wo_hbm,
    state_out, vel_out,
    grid, wq, wk, wv, wo, aug, state, q2, flat, acc, top,
    wsem, zs, zr, ps, pr, cs, cr,
):
    c = lax.axis_index("span")
    t = lax.axis_index("tok")
    zhi = c // 2
    core = c % 2
    y = t // 16
    zl = (t // 4) % 4
    x = t % 4
    upper = zhi == 1

    def tok(yy, zz, xx):
        return yy * 16 + zz * 4 + xx

    def plane_peer(place):
        return c, tok((y + place[0]) % 4, zl, (x + place[1]) % 4)

    across_z = (1 - zhi) * 2 + core
    mate = (zhi * 2 + 1 - core, t)

    loads = [
        pltpu.make_async_copy(wk_hbm, wk.at[pl.ds(0, CHANS), :], wsem.at[0]),
        pltpu.make_async_copy(wq_hbm, wq.at[pl.ds(0, CHANS), :], wsem.at[1]),
        pltpu.make_async_copy(wv_hbm, wv.at[pl.ds(0, CHANS), :], wsem.at[2]),
        pltpu.make_async_copy(wo_hbm, wo, wsem.at[3]),
    ]
    for item in loads:
        item.start()

    barrier = pltpu.get_barrier_semaphore()

    def greet(dev):
        pl.semaphore_signal(barrier, inc=1, device_id=dev, device_id_type=MESH)

    for d in range(1, 4):
        greet((c, tok(y, (zl + d) % 4, x)))
    for d in range(4):
        greet((across_z, tok(y, d, x)))
    for place in PLACES[1:]:
        greet(plane_peer(place))
    greet(mate)

    lane = lax.broadcasted_iota(jnp.int32, (1, 128), 1)
    row16 = lax.broadcasted_iota(jnp.int32, (16, WIDTH), 0)
    for which, ref in enumerate((wq, wk, wv)):
        cvec = cond_ref[which : which + 1, :]
        chi = cvec.astype(BF).astype(F32)
        clo = cvec - chi
        rows = jnp.where((row16 == 0) | (row16 == 2), chi, jnp.where(row16 == 1, clo, 0.0))
        ref[CHANS : CHANS + 16, :] = rows.astype(BF)
        ref[CHANS + 16 :, :] = jnp.zeros((128 - CHANS - 16, WIDTH), BF)
    gk = jnp.zeros((1, 128), F32)
    for h in range(HEADS):
        gk = jnp.where((lane == CHANS + h) | (lane == CHANS + HEADS + h), gain_ref[1, h], gk)
    gk = gk * (HD ** (-0.5) * LOG2E)
    down = lax.broadcasted_iota(jnp.int32, (128, 128), 0)
    across = lax.broadcasted_iota(jnp.int32, (128, 128), 1)
    spread = jnp.where((down >= CHANS) & (down % HEADS == across % HEADS), 1.0, 0.0).astype(BF)
    eye = jnp.where(down == across, 1.0, 0.0).astype(BF)
    pmask = jnp.where(lane < CHANS, 1.0, 0.0)
    state[...] = jnp.zeros_like(state)
    state[:, 0:CHANS] = latent_ref[...]

    def sigma(span, extra):
        level = jnp.full((1, 128), step_ref[span] + extra, jnp.int32).astype(F32)
        frac = 1.0 - level / NSTEPS
        return 3.0 * frac / (1.0 + 2.0 * frac)

    def rdma(src, dst, send, recv, dev):
        return pltpu.make_async_remote_copy(
            src_ref=src, dst_ref=dst, send_sem=send, recv_sem=recv, device_id=dev, device_id_type=MESH
        )

    def drain(ref, sem):
        pltpu.make_async_copy(ref, ref, sem).wait()

    loads[0].wait()

    def step(s, carry):
        def rows_of(e, at, count):
            return grid.at[s, e, pl.ds(at, count), :]

        def chunk_of(e, g):
            at = pl.multiple_of(g * CHUNK, CHUNK)
            return grid.at[s, e, pl.ds(at, CHUNK), :]

        for span in range(4):
            sig = sigma(span, s)
            shi = sig.astype(BF).astype(F32)
            slo = sig - shi
            line = jnp.where(
                (lane == CHANS) | (lane == CHANS + 1),
                shi,
                jnp.where(lane == CHANS + 2, slo, jnp.where(lane == CHANS + 3, 1.0, 0.0)),
            )
            aug[span] = jnp.broadcast_to(line, (8, 128))
        patches = state[...]
        own = (patches + aug[c][0:1, :]).astype(BF)

        squares = jnp.zeros((ROWS, 128), F32)
        pk = dot_nn(own, wk[...])
        for h in range(HEADS):
            part = pk[:, h * HD : (h + 1) * HD]
            ms = jnp.sum(part * part, axis=-1, keepdims=True)
            squares = jnp.where((lane == CHANS + h) | (lane == CHANS + HEADS + h), ms, squares)
        factor = gk / jnp.sqrt(squares * (1.0 / HD) + 1e-06)
        fhi = factor.astype(BF).astype(F32)
        row = jnp.where(lane < CHANS, patches, jnp.where(lane < CHANS + HEADS, fhi, factor - fhi)).astype(BF)
        at = pl.multiple_of(zl * ROWS, ROWS)
        grid[s, c, pl.ds(at, ROWS), :] = row

        @pl.when(s == 0)
        def _():
            pl.semaphore_wait(barrier, 23)

        block = rows_of(c, at, ROWS)
        for d in range(1, 4):
            rdma(block, block, zs.at[s], zr.at[s, zhi], (c, tok(y, (zl + d) % 4, x))).start()

        @pl.when(jnp.logical_not(upper))
        def _():
            for d in range(4):
                rdma(block, block, zs.at[s], zr.at[s, 0], (across_z, tok(y, d, x))).start()

        def spread_plane(ss, r):
            e = core + 2 * r
            for place in PLACES[1:]:
                slot = SLOT[(-place[0] % 4, -place[1] % 4)]
                rdma(
                    grid.at[ss, e, pl.ds(0, PIECE), :],
                    grid.at[ss, e, pl.ds(slot * PIECE, PIECE), :],
                    ps.at[ss, r],
                    pr.at[ss, r, slot // 4],
                    plane_peer(place),
                ).start()

        def own_plane():
            drain(rows_of(0, 0, 3 * ROWS), zr.at[s, zhi])
            spread_plane(s, zhi)

        def lower_plane(ss):
            drain(rows_of(0, 0, 4 * ROWS), zr.at[ss, 0])
            spread_plane(ss, 0)

        @pl.when(s == 0)
        def _():
            loads[1].wait()

        pq = dot_nn(own, wq[...])
        normed = []
        for h in range(HEADS):
            part = pq[:, h * HD : (h + 1) * HD]
            ms = jnp.sum(part * part, axis=-1, keepdims=True) * (1.0 / HD)
            normed.append((part / jnp.sqrt(ms + 1e-06) * gain_ref[0, h]).astype(BF))
        for h in range(HEADS):
            flat[pl.ds(h, ROWS, stride=HEADS), :] = dot_nt(normed[h], wk[:, h * HD : (h + 1) * HD])
        qk = flat[...]
        qhi = qk.astype(BF)
        q2[:, 0:128] = qhi
        q2[:, 128:256] = (qk - qhi.astype(F32)).astype(BF)
        acc[...] = jnp.zeros_like(acc)
        top[...] = jnp.full_like(top, -1e30)
        late = (s == 1) & (c == 3)

        @pl.when(jnp.logical_not(late))
        def _():
            own_plane()

        @pl.when(upper & (s == 0))
        def _():
            lower_plane(0)

        def attend(blocks):
            keys, factors, turned = [], [], []
            for e, g in blocks:
                rows = chunk_of(e, g)[...]
                plain = rows * pmask.astype(BF) + aug[e][0:1, :].astype(BF)
                keys.append(jnp.concatenate([plain, plain], axis=1))
                factors.append(dot_nn(rows, spread))
                turned.append(dot_nt(eye, plain).astype(BF))
            units = [(b, slice(u * COLS, (u + 1) * COLS)) for b in range(len(blocks)) for u in range(QUERIES // COLS)]

            def score(n):
                b, cols = units[n]
                return dot_nt(keys[b], q2[cols, :])

            def soften(n, raw):
                b, cols = units[n]
                scaled, best = [], None
                for at in range(0, CHUNK, SUB):
                    wide = jnp.concatenate([factors[b][at : at + SUB, :]] * (COLS // 128), axis=1)
                    part = raw[at : at + SUB, :] * wide
                    scaled.append(part)
                    high = jnp.max(part.reshape(SUB // 8, 8, COLS), axis=0)
                    best = high if best is None else jnp.maximum(best, high)
                old = top[0:1, cols]
                new = jnp.maximum(old, jnp.max(best, axis=0, keepdims=True))
                top[0:1, cols] = new
                weights = [jnp.exp2(part - new).astype(BF) for part in scaled]
                return n, jnp.concatenate(weights, axis=0), jnp.exp2(old - new)

            def gather(n, weights, alpha):
                b, cols = units[n]
                acc[:, cols] = acc[:, cols] * alpha + dot_nn(turned[b], weights)

            raw = score(0)
            pending = []
            for n in range(len(units)):
                later = score(n + 1) if n + 1 < len(units) else None
                pending.append(soften(n, raw))
                raw = later
                if len(pending) > LAG:
                    gather(*pending.pop(0))
            for item in pending:
                gather(*item)

        three = (s == 0) & (c == 2)
        count = jnp.where(three, 3, 4)

        def place_of(m, q):
            e = jnp.where(s == 0, jnp.where(three, q, q % (c + 1)), m)
            g = jnp.where(s == 0, jnp.where(three, m, (4 * m + q) // (c + 1)), q)
            return e, g

        def group(m, carry):
            def arrive(q, carry):
                e, g = place_of(m, q)
                r = e // 2

                @pl.when(e % 2 == core)
                def _():
                    @pl.when(g == 0)
                    def _():
                        drain(rows_of(0, 0, 3 * PIECE), pr.at[s, r, g])

                    @pl.when(g > 0)
                    def _():
                        drain(rows_of(0, 0, 4 * PIECE), pr.at[s, r, g])

                    @pl.when(r <= zhi - core)
                    def _():
                        ref = chunk_of(e, g)
                        rdma(ref, ref, cs.at[s, r], cr.at[s, r, g], mate).start()

                return carry

            def cross(q, carry):
                e, g = place_of(m, q)

                @pl.when(e % 2 != core)
                def _():
                    drain(rows_of(0, 0, CHUNK), cr.at[s, e // 2, g])

                return carry

            lax.fori_loop(0, count, arrive, 0)
            lax.fori_loop(0, count, cross, 0)

            @pl.when(three)
            def _():
                attend([place_of(m, q) for q in range(3)])

            @pl.when(jnp.logical_not(three))
            def _():
                attend([place_of(m, q) for q in range(4)])

            @pl.when(late & (m == 0))
            def _():
                own_plane()

            return carry

        lax.fori_loop(0, jnp.where(three, 4, c + 1), group, 0)

        @pl.when(upper & (s == 0))
        def _():
            lower_plane(1)

        @pl.when(s == 0)
        def _():
            loads[2].wait()
            loads[3].wait()

        sums = acc[...]
        flat[...] = (sums / sums[CHANS + 3 : CHANS + 4, :]).T
        attended = []
        for h in range(HEADS):
            zed = flat[pl.ds(h, ROWS, stride=HEADS), :]
            zed_hi = zed.astype(BF)
            zed_lo = (zed - zed_hi.astype(F32)).astype(BF)
            both = dot_nn(jnp.concatenate([zed_hi, zed_lo], axis=0), wv[:, h * HD : (h + 1) * HD])
            attended.append((both[0:ROWS] + both[ROWS:]).astype(BF))
        velocity = dot_nt(jnp.concatenate(attended, axis=1), wo[...])
        change = sigma(c, s + 1) - sigma(c, s)
        state[:, 0:CHANS] = state[:, 0:CHANS] + change[:, 0:CHANS] * velocity
        vel_out[...] = velocity
        return carry

    lax.fori_loop(0, 2, step, 0)
    state_out[...] = state[:, 0:CHANS]

    def finish(s, carry):
        @pl.when(upper)
        def _():
            drain(grid.at[0, 0, pl.ds(0, 3 * ROWS), :], zs.at[s])

        @pl.when(jnp.logical_not(upper))
        def _():
            drain(grid.at[0, 0, pl.ds(0, 7 * ROWS), :], zs.at[s])

        def rail(r, carry):
            drain(grid.at[0, 0, pl.ds(0, 15 * PIECE), :], ps.at[s, r])

            @pl.when(r <= zhi - core)
            def _():
                drain(grid.at[0, 0], cs.at[s, r])

            return carry

        lax.fori_loop(0, zhi + 1, rail, 0)
        return carry

    lax.fori_loop(0, 2, finish, 0)


def local(latent, step_index, w_query, w_key, w_value, cond, qk_gain, w_out):
    vmem = pl.BlockSpec(memory_space=pltpu.VMEM)
    smem = pl.BlockSpec(memory_space=pltpu.SMEM)
    hbm = pl.BlockSpec(memory_space=pl.ANY)
    dma = pltpu.SemaphoreType.DMA
    out = jax.ShapeDtypeStruct((ROWS, CHANS), F32)
    state, velocity = pl.pallas_call(
        kernel,
        out_shape=(out, out),
        in_specs=[smem, smem, vmem, vmem, hbm, hbm, hbm, hbm],
        out_specs=(vmem, vmem),
        scratch_shapes=[
            pltpu.VMEM((2, 4, SEQ, 128), BF),
            pltpu.VMEM((128, WIDTH), BF),
            pltpu.VMEM((128, WIDTH), BF),
            pltpu.VMEM((128, WIDTH), BF),
            pltpu.VMEM((CHANS, WIDTH), BF),
            pltpu.VMEM((4, 8, 128), F32),
            pltpu.VMEM((ROWS, 128), F32),
            pltpu.VMEM((QUERIES, 256), BF),
            pltpu.VMEM((QUERIES, 128), F32),
            pltpu.VMEM((128, QUERIES), F32),
            pltpu.VMEM((8, QUERIES), F32),
            dma((4,)),
            dma((2,)),
            dma((2, 2)),
            dma((2, 2)),
            dma((2, 2, 4)),
            dma((2, 2)),
            dma((2, 2, 4)),
        ],
        compiler_params=pltpu.CompilerParams(
            collective_id=0, has_side_effects=True, vmem_limit_bytes=63 * 1024 * 1024
        ),
    )(step_index, qk_gain, latent[0], cond, w_query, w_key, w_value, w_out.T)
    return state[None], velocity[None]


def solution(mesh):
    return jax.shard_map(
        local,
        mesh=mesh,
        in_specs=(P("span", "tok", None), P(), P(), P(), P(), P(), P(), P()),
        out_specs=(P("span", "tok", None), P("span", "tok", None)),
        check_vma=False,
    )
```

```python
import jax
import jax.numpy as jnp
from jax import lax
from jax.experimental import pallas as pl
from jax.experimental.pallas import tpu as pltpu
from jax.sharding import PartitionSpec as P

MESH = pl.DeviceIdType.MESH
NSTEPS = 8
ROWS = 32
PIECE = 4 * ROWS
CHANS = 64
HEADS = 32
HD = 128
WIDTH = HEADS * HD
SEQ = 2048
CHUNK = SEQ // 4
QUERIES = HEADS * ROWS
COLS = QUERIES // 2
SUB = 64
LAG = 2
PLACES = (
    (0, 0), (1, 0), (3, 0), (0, 1), (0, 3), (1, 1), (3, 3), (1, 3),
    (3, 1), (2, 0), (0, 2), (2, 1), (2, 3), (1, 2), (3, 2), (2, 2),
)
WHOLE = [[(e, g) for g in range(4)] for e in range(4)]
GROUPS = (
    (
        [[(0, 0), (0, 1)], [(0, 2), (0, 3)]],
        [[(1, 0), (1, 1), (0, 0), (0, 1)], [(1, 2), (1, 3), (0, 2), (0, 3)]],
        [[(2, 0), (0, 0), (2, 1), (0, 1)], [(2, 2), (0, 2), (1, 0), (1, 1)], [(2, 3), (0, 3), (1, 2), (1, 3)]],
        [
            [(3, 0), (1, 0), (3, 1), (1, 1)],
            [(2, 0), (0, 0), (2, 1), (0, 1)],
            [(3, 2), (1, 2), (2, 2), (0, 2)],
            [(3, 3), (1, 3), (2, 3), (0, 3)],
        ],
    ),
    (
        [[(0, 0), (0, 1)], [(0, 2), (0, 3)]],
        [WHOLE[0], WHOLE[1]],
        [WHOLE[0], WHOLE[1], WHOLE[2]],
        [WHOLE[0], WHOLE[1], [(3, 0), (3, 1), (2, 0), (2, 1)], [(3, 2), (3, 3), (2, 2), (2, 3)]],
    ),
)
AHEAD = {(1, 2, 1): [(2, 0), (2, 1)]}
LOG2E = 1.4426950408889634
BF = jnp.bfloat16
F32 = jnp.float32


def dot_nt(a, b):
    return lax.dot_general(a, b, (((1,), (1,)), ((), ())), preferred_element_type=F32)


def dot_nn(a, b):
    return jnp.dot(a, b, preferred_element_type=F32)


def kernel(
    step_ref, gain_ref, latent_ref, cond_ref, wq_hbm, wk_hbm, wv_hbm, wo_hbm,
    out_ref,
    grid, wq, wk, wv, wo, aug, state, q2, flat, acc, top,
    wsem, zs, zr, ps, pr, cs, cr,
):
    c = lax.axis_index("span")
    t = lax.axis_index("tok")
    zhi = c >> 1
    core = c & 1
    y = t >> 4
    zl = (t >> 2) & 3
    x = t & 3
    upper = zhi == 1

    def tok(yy, zz, xx):
        return (yy << 4) | (zz << 2) | xx

    def plane_peer(place):
        return c, tok((y + place[0]) & 3, zl, (x + place[1]) & 3)

    across_z = (1 - zhi) * 2 + core
    mate = (zhi * 2 + 1 - core, t)

    loads = [
        pltpu.make_async_copy(wk_hbm, wk.at[pl.ds(0, CHANS), :], wsem.at[0]),
        pltpu.make_async_copy(wq_hbm, wq.at[pl.ds(0, CHANS), :], wsem.at[1]),
        pltpu.make_async_copy(wv_hbm, wv.at[pl.ds(0, CHANS), :], wsem.at[2]),
        pltpu.make_async_copy(wo_hbm, wo, wsem.at[3]),
    ]
    for item in loads:
        item.start()

    barrier = pltpu.get_barrier_semaphore()

    def greet(dev):
        pl.semaphore_signal(barrier, inc=1, device_id=dev, device_id_type=MESH)

    for d in range(1, 4):
        greet((c, tok(y, (zl + d) & 3, x)))
    for d in range(4):
        greet((across_z, tok(y, d, x)))
    for place in PLACES[1:]:
        greet(plane_peer(place))
    greet(mate)

    lane = lax.broadcasted_iota(jnp.int32, (1, 128), 1)
    row16 = lax.broadcasted_iota(jnp.int32, (16, WIDTH), 0)
    for which, ref in enumerate((wq, wk, wv)):
        cvec = cond_ref[which : which + 1, :]
        chi = cvec.astype(BF).astype(F32)
        clo = cvec - chi
        rows = jnp.where((row16 == 0) | (row16 == 2), chi, jnp.where(row16 == 1, clo, 0.0))
        ref[CHANS : CHANS + 16, :] = rows.astype(BF)
        ref[CHANS + 16 :, :] = jnp.zeros((128 - CHANS - 16, WIDTH), BF)
    gk = jnp.zeros((1, 128), F32)
    for h in range(HEADS):
        gk = jnp.where((lane == CHANS + h) | (lane == CHANS + HEADS + h), gain_ref[1, h], gk)
    gk = gk * (HD ** (-0.5) * LOG2E)
    down = lax.broadcasted_iota(jnp.int32, (128, 128), 0)
    across = lax.broadcasted_iota(jnp.int32, (128, 128), 1)
    spread = jnp.where((down >= CHANS) & (down % HEADS == across % HEADS), 1.0, 0.0).astype(BF)
    eye = jnp.where(down == across, 1.0, 0.0).astype(BF)
    pmask = jnp.where(lane < CHANS, 1.0, 0.0)
    state[...] = jnp.zeros_like(state)
    state[:, 0:CHANS] = latent_ref[...]

    def sigma(span, extra):
        level = jnp.full((1, 128), step_ref[span] + extra, jnp.int32).astype(F32)
        frac = 1.0 - level / NSTEPS
        return 3.0 * frac / (1.0 + 2.0 * frac)

    def rdma(src, dst, send, recv, dev):
        return pltpu.make_async_remote_copy(
            src_ref=src, dst_ref=dst, send_sem=send, recv_sem=recv, device_id=dev, device_id_type=MESH
        )

    def drain(ref, sem):
        pltpu.make_async_copy(ref, ref, sem).wait()

    loads[0].wait()

    def step(s, carry):
        def rows_of(e, at, count):
            return grid.at[s, e, pl.ds(at, count), :]

        def chunk_of(e, g):
            at = pl.multiple_of(g * CHUNK, CHUNK)
            return grid.at[s, e, pl.ds(at, CHUNK), :]

        for span in range(4):
            sig = sigma(span, s)
            shi = sig.astype(BF).astype(F32)
            slo = sig - shi
            line = jnp.where(
                (lane == CHANS) | (lane == CHANS + 1),
                shi,
                jnp.where(lane == CHANS + 2, slo, jnp.where(lane == CHANS + 3, 1.0, 0.0)),
            )
            aug[span] = jnp.broadcast_to(line, (8, 128))
        patches = state[...]
        own = (patches + aug[c][0:1, :]).astype(BF)

        squares = jnp.zeros((ROWS, 128), F32)
        pk = dot_nn(own, wk[...])
        for h in range(HEADS):
            part = pk[:, h * HD : (h + 1) * HD]
            ms = jnp.sum(part * part, axis=-1, keepdims=True)
            squares = jnp.where((lane == CHANS + h) | (lane == CHANS + HEADS + h), ms, squares)
        factor = gk / jnp.sqrt(squares * (1.0 / HD) + 1e-06)
        fhi = factor.astype(BF).astype(F32)
        row = jnp.where(lane < CHANS, patches, jnp.where(lane < CHANS + HEADS, fhi, factor - fhi)).astype(BF)
        at = pl.multiple_of(zl * ROWS, ROWS)
        grid[s, c, pl.ds(at, ROWS), :] = row

        @pl.when(s == 0)
        def _():
            pl.semaphore_wait(barrier, 23)

        block = rows_of(c, at, ROWS)
        for d in range(1, 4):
            rdma(block, block, zs.at[s], zr.at[s, zhi], (c, tok(y, (zl + d) & 3, x))).start()

        @pl.when(jnp.logical_not(upper))
        def _():
            for d in range(4):
                rdma(block, block, zs.at[s], zr.at[s, 0], (across_z, tok(y, d, x))).start()

        def send_chunk(ss, r, g):
            e = core + 2 * r
            for slot in range(max(4 * g, 1), 4 * g + 4):
                rdma(
                    grid.at[ss, e, pl.ds(0, PIECE), :],
                    grid.at[ss, e, pl.ds(slot * PIECE, PIECE), :],
                    ps.at[ss, r, g],
                    pr.at[ss, r, g],
                    plane_peer((-PLACES[slot][0], -PLACES[slot][1])),
                ).start()

        def own_plane():
            drain(rows_of(0, 0, 3 * ROWS), zr.at[s, zhi])
            for g in range(4):
                send_chunk(s, zhi, g)

        def lower_plane(ss):
            drain(rows_of(0, 0, 4 * ROWS), zr.at[ss, 0])
            for g in range(4):
                send_chunk(ss, 0, g)

        @pl.when(s == 0)
        def _():
            loads[1].wait()

        pq = dot_nn(own, wq[...])
        normed = []
        for h in range(HEADS):
            part = pq[:, h * HD : (h + 1) * HD]
            ms = jnp.sum(part * part, axis=-1, keepdims=True) * (1.0 / HD)
            normed.append((part / jnp.sqrt(ms + 1e-06) * gain_ref[0, h]).astype(BF))
        for h in range(HEADS):
            flat[pl.ds(h, ROWS, stride=HEADS), :] = dot_nt(normed[h], wk[:, h * HD : (h + 1) * HD])
        qk = flat[...]
        qhi = qk.astype(BF)
        q2[:, 0:128] = qhi
        q2[:, 128:256] = (qk - qhi.astype(F32)).astype(BF)
        acc[...] = jnp.zeros_like(acc)
        top[...] = jnp.full_like(top, -1e30)
        @pl.when(jnp.logical_not(upper) | (s == 1))
        def _():
            own_plane()

        @pl.when(upper & (s == 0))
        def _():
            drain(rows_of(0, 0, 3 * ROWS), zr.at[s, 1])
            drain(rows_of(0, 0, 4 * ROWS), zr.at[s, 0])
            for g in range(4):
                for r in range(2):
                    send_chunk(s, r, g)

        def attend(blocks):
            keys, factors, turned = [], [], []
            for e, g in blocks:
                rows = chunk_of(e, g)[...]
                plain = rows * pmask.astype(BF) + aug[e][0:1, :].astype(BF)
                keys.append(jnp.concatenate([plain, plain], axis=1))
                factors.append(dot_nn(rows, spread))
                turned.append(dot_nt(eye, plain).astype(BF))
            units = [(b, slice(u * COLS, (u + 1) * COLS)) for b in range(len(blocks)) for u in range(QUERIES // COLS)]

            def score(n):
                b, cols = units[n]
                return dot_nt(keys[b], q2[cols, :])

            def soften(n, raw):
                b, cols = units[n]
                scaled, best = [], None
                for at in range(0, CHUNK, SUB):
                    wide = jnp.concatenate([factors[b][at : at + SUB, :]] * (COLS // 128), axis=1)
                    part = raw[at : at + SUB, :] * wide
                    scaled.append(part)
                    high = jnp.max(part.reshape(SUB // 8, 8, COLS), axis=0)
                    best = high if best is None else jnp.maximum(best, high)
                old = top[0:1, cols]
                new = jnp.maximum(old, jnp.max(best, axis=0, keepdims=True))
                top[0:1, cols] = new
                weights = [jnp.exp2(part - new).astype(BF) for part in scaled]
                return n, jnp.concatenate(weights, axis=0), jnp.exp2(old - new)

            def gather(n, weights, alpha):
                b, cols = units[n]
                acc[:, cols] = acc[:, cols] * alpha + dot_nn(turned[b], weights)

            raw = score(0)
            pending = []
            for n in range(len(units)):
                later = score(n + 1) if n + 1 < len(units) else None
                pending.append(soften(n, raw))
                raw = later
                if len(pending) > LAG:
                    gather(*pending.pop(0))
            for item in pending:
                gather(*item)

        def group(m, carry):
            key = s * 16 + c * 4 + m
            code = jnp.int32(0)
            for ss in range(2):
                for cc in range(4):
                    for mm, chunks in enumerate(GROUPS[ss][cc]):
                        here = key == ss * 16 + cc * 4 + mm
                        packed = sum((4 * e + g) << (4 * q) for q, (e, g) in enumerate(chunks))
                        code = jnp.where(here, packed, code)

                        @pl.when(here)
                        def _(ss=ss, cc=cc, mm=mm, chunks=chunks):
                            for e, g in chunks + AHEAD.get((ss, cc, mm), []):
                                r = e // 2
                                if e % 2 == cc % 2 and (e, g) not in AHEAD.get((ss, cc, mm - 1), []):
                                    drain(rows_of(0, 0, (4 if g else 3) * PIECE), pr.at[ss, r, g])
                                    if r <= cc // 2 - cc % 2:
                                        ref = grid.at[ss, e, pl.ds(g * CHUNK, CHUNK), :]
                                        rdma(ref, ref, cs.at[ss, r], cr.at[ss, r, g], mate).start()
                            for e, g in chunks:
                                if e % 2 != cc % 2:
                                    drain(rows_of(0, 0, CHUNK), cr.at[ss, e // 2, g])

            @pl.when((s == 0) & (c == 2) & (m == 2))
            def _():
                lower_plane(1)

            blocks = [((code >> (4 * q + 2)) & 3, (code >> (4 * q)) & 3) for q in range(4)]

            @pl.when(c == 0)
            def _():
                attend(blocks[:2])

            @pl.when(c > 0)
            def _():
                attend(blocks)

            return carry

        lax.fori_loop(0, jnp.maximum(c + 1, 2), group, 0)

        @pl.when((s == 0) & (c == 3))
        def _():
            lower_plane(1)

        @pl.when(s == 0)
        def _():
            loads[2].wait()
            loads[3].wait()

        sums = acc[...]
        flat[...] = (sums / sums[CHANS + 3 : CHANS + 4, :]).T
        attended = []
        for h in range(HEADS):
            zed = flat[pl.ds(h, ROWS, stride=HEADS), :]
            zed_hi = zed.astype(BF)
            zed_lo = (zed - zed_hi.astype(F32)).astype(BF)
            both = dot_nn(jnp.concatenate([zed_hi, zed_lo], axis=0), wv[:, h * HD : (h + 1) * HD])
            attended.append((both[0:ROWS] + both[ROWS:]).astype(BF))
        velocity = dot_nt(jnp.concatenate(attended, axis=1), wo[...])
        change = sigma(c, s + 1) - sigma(c, s)
        state[:, 0:CHANS] = state[:, 0:CHANS] + change[:, 0:CHANS] * velocity
        out_ref[1] = velocity
        return carry

    lax.fori_loop(0, 2, step, 0)
    out_ref[0] = state[:, 0:CHANS]

    def finish(s, carry):
        @pl.when(upper)
        def _():
            drain(grid.at[0, 0, pl.ds(0, 3 * ROWS), :], zs.at[s])

        @pl.when(jnp.logical_not(upper))
        def _():
            drain(grid.at[0, 0, pl.ds(0, 7 * ROWS), :], zs.at[s])

        def rail(r, carry):
            for g in range(4):
                drain(grid.at[0, 0, pl.ds(0, (4 if g else 3) * PIECE), :], ps.at[s, r, g])

            @pl.when(r <= zhi - core)
            def _():
                drain(grid.at[0, 0], cs.at[s, r])

            return carry

        lax.fori_loop(0, zhi + 1, rail, 0)
        return carry

    lax.fori_loop(0, 2, finish, 0)


def local(latent, step_index, w_query, w_key, w_value, cond, qk_gain, w_out):
    vmem = pl.BlockSpec(memory_space=pltpu.VMEM)
    smem = pl.BlockSpec(memory_space=pltpu.SMEM)
    hbm = pl.BlockSpec(memory_space=pl.ANY)
    dma = pltpu.SemaphoreType.DMA
    both = pl.pallas_call(
        kernel,
        out_shape=jax.ShapeDtypeStruct((2, ROWS, CHANS), F32),
        in_specs=[smem, smem, vmem, vmem, hbm, hbm, hbm, hbm],
        out_specs=vmem,
        scratch_shapes=[
            pltpu.VMEM((2, 4, SEQ, 128), BF),
            pltpu.VMEM((128, WIDTH), BF),
            pltpu.VMEM((128, WIDTH), BF),
            pltpu.VMEM((128, WIDTH), BF),
            pltpu.VMEM((CHANS, WIDTH), BF),
            pltpu.VMEM((4, 8, 128), F32),
            pltpu.VMEM((ROWS, 128), F32),
            pltpu.VMEM((QUERIES, 256), BF),
            pltpu.VMEM((QUERIES, 128), F32),
            pltpu.VMEM((128, QUERIES), F32),
            pltpu.VMEM((8, QUERIES), F32),
            dma((4,)),
            dma((2,)),
            dma((2, 2)),
            dma((2, 2, 4)),
            dma((2, 2, 4)),
            dma((2, 2)),
            dma((2, 2, 4)),
        ],
        compiler_params=pltpu.CompilerParams(
            collective_id=0, has_side_effects=True, vmem_limit_bytes=63 * 1024 * 1024
        ),
    )(step_index, qk_gain, latent[0], cond, w_query, w_key, w_value, w_out.T)
    return both[0:1], both[1:2]


def solution(mesh):
    return jax.shard_map(
        local,
        mesh=mesh,
        in_specs=(P("span", "tok", None), P(), P(), P(), P(), P(), P(), P()),
        out_specs=(P("span", "tok", None), P("span", "tok", None)),
        check_vma=False,
    )
```

```python
import jax
import jax.numpy as jnp
from jax import lax
from jax.experimental import pallas as pl
from jax.experimental.pallas import tpu as pltpu
from jax.sharding import PartitionSpec as P

MESH = pl.DeviceIdType.MESH
NSTEPS = 8
ROWS = 32
PIECE = 4 * ROWS
CHANS = 64
HEADS = 32
HD = 128
WIDTH = HEADS * HD
SEQ = 2048
CHUNK = SEQ // 4
QUERIES = HEADS * ROWS
COLS = QUERIES // 4
SUB = 64
LAG = 3
PLACES = (
    (0, 0), (1, 0), (3, 0), (0, 1), (0, 3), (1, 1), (3, 3), (1, 3),
    (3, 1), (2, 0), (0, 2), (2, 1), (2, 3), (1, 2), (3, 2), (2, 2),
)
WHOLE = [[(e, g) for g in range(4)] for e in range(4)]
GROUPS = (
    (
        [[(0, 0), (0, 1)], [(0, 2), (0, 3)]],
        [[(1, 0), (1, 1), (0, 0), (0, 1)], [(1, 2), (1, 3), (0, 2), (0, 3)]],
        [[(2, 0), (0, 0), (2, 1), (0, 1)], [(2, 2), (0, 2), (1, 0), (1, 1)], [(2, 3), (0, 3), (1, 2), (1, 3)]],
        [
            [(3, 0), (1, 0), (3, 1), (1, 1)],
            [(2, 0), (0, 0), (2, 1), (0, 1)],
            [(3, 2), (1, 2), (2, 2), (0, 2)],
            [(3, 3), (1, 3), (2, 3), (0, 3)],
        ],
    ),
    (
        [[(0, 0), (0, 1)], [(0, 2), (0, 3)]],
        [WHOLE[0], WHOLE[1]],
        [WHOLE[0], WHOLE[1], [(2, 0), (2, 1)], [(2, 2), (2, 3)]],
        [WHOLE[1], WHOLE[0], [(3, 0), (3, 1), (2, 0), (2, 1)], [(3, 2), (2, 2)], [(3, 3), (2, 3)]],
    ),
)
AHEAD = {(1, 2, 1): [(2, 0), (2, 1)], (1, 2, 2): [(2, 2), (2, 3)]}
LOG2E = 1.4426950408889634
BF = jnp.bfloat16
F32 = jnp.float32


def dot_nt(a, b):
    return lax.dot_general(a, b, (((1,), (1,)), ((), ())), preferred_element_type=F32)


def dot_nn(a, b):
    return jnp.dot(a, b, preferred_element_type=F32)


def kernel(
    step_ref, gain_ref, latent_hbm, cond_hbm, wq_hbm, wk_hbm, wv_hbm, wo_hbm,
    out_ref,
    grid, latent_ref, cond_ref, wq, wk, wv, wo, aug, state, q2, flat, acc, top,
    wsem, zs, zr, ps, pr, cs, cr,
):
    c = lax.axis_index("span")
    t = lax.axis_index("tok")
    zhi = c >> 1
    core = c & 1
    y = t >> 4
    zl = (t >> 2) & 3
    x = t & 3
    upper = zhi == 1

    def tok(yy, zz, xx):
        return (yy << 4) | (zz << 2) | xx

    def plane_peer(place):
        return c, tok((y + place[0]) & 3, zl, (x + place[1]) & 3)

    across_z = (1 - zhi) * 2 + core
    mate = (zhi * 2 + 1 - core, t)

    barrier = pltpu.get_barrier_semaphore()

    def greet(dev):
        pl.semaphore_signal(barrier, inc=1, device_id=dev, device_id_type=MESH)

    for d in range(1, 4):
        greet((c, tok(y, (zl + d) & 3, x)))
    for d in range(4):
        greet((across_z, tok(y, d, x)))
    for place in PLACES[1:]:
        greet(plane_peer(place))
    greet(mate)

    loads = [
        pltpu.make_async_copy(wk_hbm, wk.at[pl.ds(0, CHANS), :], wsem.at[0]),
        pltpu.make_async_copy(wq_hbm, wq.at[pl.ds(0, CHANS), :], wsem.at[1]),
        pltpu.make_async_copy(wv_hbm, wv.at[pl.ds(0, CHANS), :], wsem.at[2]),
        pltpu.make_async_copy(wo_hbm, wo, wsem.at[3]),
        pltpu.make_async_copy(cond_hbm, cond_ref, wsem.at[4]),
        pltpu.make_async_copy(latent_hbm, latent_ref, wsem.at[5]),
    ]
    for n in (4, 0, 5, 1, 2, 3):
        loads[n].start()

    lane = lax.broadcasted_iota(jnp.int32, (1, 128), 1)
    loads[4].wait()
    row16 = lax.broadcasted_iota(jnp.int32, (16, WIDTH), 0)
    for which, ref in enumerate((wq, wk, wv)):
        cvec = cond_ref[which : which + 1, :]
        chi = cvec.astype(BF).astype(F32)
        clo = cvec - chi
        rows = jnp.where((row16 == 0) | (row16 == 2), chi, jnp.where(row16 == 1, clo, 0.0))
        ref[CHANS : CHANS + 16, :] = rows.astype(BF)
        ref[CHANS + 16 :, :] = jnp.zeros((128 - CHANS - 16, WIDTH), BF)
    gk = jnp.zeros((1, 128), F32)
    for h in range(HEADS):
        gk = jnp.where((lane == CHANS + h) | (lane == CHANS + HEADS + h), gain_ref[1, h], gk)
    gk = gk * (HD ** (-0.5) * LOG2E)
    down = lax.broadcasted_iota(jnp.int32, (128, 128), 0)
    across = lax.broadcasted_iota(jnp.int32, (128, 128), 1)
    spread = jnp.where((down >= CHANS) & (down % HEADS == across % HEADS), 1.0, 0.0).astype(BF)
    eye = jnp.where(down == across, 1.0, 0.0).astype(BF)
    pmask = jnp.where(lane < CHANS, 1.0, 0.0)
    state[...] = jnp.zeros_like(state)
    loads[5].wait()
    state[:, 0:CHANS] = latent_ref[...]

    def sigma(span, extra):
        level = jnp.full((1, 128), step_ref[span] + extra, jnp.int32).astype(F32)
        frac = 1.0 - level / NSTEPS
        return 3.0 * frac / (1.0 + 2.0 * frac)

    def rdma(src, dst, send, recv, dev):
        return pltpu.make_async_remote_copy(
            src_ref=src, dst_ref=dst, send_sem=send, recv_sem=recv, device_id=dev, device_id_type=MESH
        )

    def drain(ref, sem):
        pltpu.make_async_copy(ref, ref, sem).wait()

    loads[0].wait()

    def step(s, carry):
        def rows_of(e, at, count):
            return grid.at[s, e, pl.ds(at, count), :]

        def chunk_of(e, g):
            at = pl.multiple_of(g * CHUNK, CHUNK)
            return grid.at[s, e, pl.ds(at, CHUNK), :]

        for span in range(4):
            sig = sigma(span, s)
            shi = sig.astype(BF).astype(F32)
            slo = sig - shi
            line = jnp.where(
                (lane == CHANS) | (lane == CHANS + 1) | (lane == CHANS + 4),
                shi,
                jnp.where(lane == CHANS + 2, slo, jnp.where(lane == CHANS + 3, 1.0, 0.0)),
            )
            aug[span] = jnp.broadcast_to(line, (8, 128))
        patches = state[...]
        own = (patches + aug[c][0:1, :]).astype(BF)

        squares = jnp.zeros((ROWS, 128), F32)
        pk = dot_nn(own, wk[...])
        for h in range(HEADS):
            part = pk[:, h * HD : (h + 1) * HD]
            ms = jnp.sum(part * part, axis=-1, keepdims=True)
            squares = jnp.where((lane == CHANS + h) | (lane == CHANS + HEADS + h), ms, squares)
        factor = gk / jnp.sqrt(squares * (1.0 / HD) + 1e-06)
        fhi = factor.astype(BF).astype(F32)
        row = jnp.where(lane < CHANS, patches, jnp.where(lane < CHANS + HEADS, fhi, factor - fhi)).astype(BF)
        at = pl.multiple_of(zl * ROWS, ROWS)
        grid[s, c, pl.ds(at, ROWS), :] = row

        @pl.when(s == 0)
        def _():
            pl.semaphore_wait(barrier, 23)

        block = rows_of(c, at, ROWS)
        for d in range(1, 4):
            rdma(block, block, zs.at[s], zr.at[s, zhi], (c, tok(y, (zl + d) & 3, x))).start()

        @pl.when(jnp.logical_not(upper))
        def _():
            for d in range(4):
                rdma(block, block, zs.at[s], zr.at[s, 0], (across_z, tok(y, d, x))).start()

        def send_chunk(ss, r, g):
            e = core + 2 * r
            for slot in range(max(4 * g, 1), 4 * g + 4):
                rdma(
                    grid.at[ss, e, pl.ds(0, PIECE), :],
                    grid.at[ss, e, pl.ds(slot * PIECE, PIECE), :],
                    ps.at[ss, r, g],
                    pr.at[ss, r, g],
                    plane_peer((-PLACES[slot][0], -PLACES[slot][1])),
                ).start()

        def own_plane():
            drain(rows_of(0, 0, 3 * ROWS), zr.at[s, zhi])
            for g in range(4):
                send_chunk(s, zhi, g)

        def lower_plane(ss):
            drain(rows_of(0, 0, 4 * ROWS), zr.at[ss, 0])
            for g in range(4):
                send_chunk(ss, 0, g)

        @pl.when(s == 0)
        def _():
            loads[1].wait()

        pq = dot_nn(own, wq[...])
        normed = []
        for h in range(HEADS):
            part = pq[:, h * HD : (h + 1) * HD]
            ms = jnp.sum(part * part, axis=-1, keepdims=True) * (1.0 / HD)
            normed.append((part / jnp.sqrt(ms + 1e-06) * gain_ref[0, h]).astype(BF))
        for h in range(HEADS):
            flat[pl.ds(h, ROWS, stride=HEADS), :] = dot_nt(normed[h], wk[:, h * HD : (h + 1) * HD])
        qk = flat[...]
        rest = pltpu.roll(qk - qk.astype(BF).astype(F32), 4, 1)
        q2[...] = jnp.where(lane == CHANS + 4, rest, qk).astype(BF)
        acc[...] = jnp.zeros_like(acc)
        top[...] = jnp.full_like(top, -1e30)
        @pl.when(jnp.logical_not(upper) | (s == 1))
        def _():
            own_plane()

        @pl.when(upper & (s == 0))
        def _():
            drain(rows_of(0, 0, 3 * ROWS), zr.at[s, 1])
            drain(rows_of(0, 0, 4 * ROWS), zr.at[s, 0])
            for g in range(4):
                for r in range(2):
                    send_chunk(s, r, g)

        def attend(blocks):
            keys, factors, turned = [], [], []
            for e, g in blocks:
                rows = chunk_of(e, g)[...]
                plain = rows * pmask.astype(BF) + aug[e][0:1, :].astype(BF)
                keys.append(plain)
                factors.append(dot_nn(rows, spread))
                turned.append(dot_nt(eye, plain).astype(BF))
            units = [(b, slice(u * COLS, (u + 1) * COLS)) for b in range(len(blocks)) for u in range(QUERIES // COLS)]

            def score(n):
                b, cols = units[n]
                return dot_nt(keys[b], q2[cols, :])

            def soften(n, raw):
                b, cols = units[n]
                scaled, best = [], None
                for at in range(0, CHUNK, SUB):
                    wide = jnp.concatenate([factors[b][at : at + SUB, :]] * (COLS // 128), axis=1)
                    part = raw[at : at + SUB, :] * wide
                    scaled.append(part)
                    high = jnp.max(part.reshape(SUB // 8, 8, COLS), axis=0)
                    best = high if best is None else jnp.maximum(best, high)
                old = top[0:1, cols]
                new = jnp.maximum(old, jnp.max(best, axis=0, keepdims=True))
                top[0:1, cols] = new
                weights = [jnp.exp2(part - new).astype(BF) for part in scaled]
                return n, jnp.concatenate(weights, axis=0), jnp.exp2(old - new)

            def gather(n, weights, alpha):
                b, cols = units[n]
                acc[:, cols] = acc[:, cols] * alpha + dot_nn(turned[b], weights)

            raw = score(0)
            pending = []
            for n in range(len(units)):
                later = score(n + 1) if n + 1 < len(units) else None
                pending.append(soften(n, raw))
                raw = later
                if len(pending) > LAG:
                    gather(*pending.pop(0))
            for item in pending:
                gather(*item)

        def group(m, carry):
            @pl.when((s == 0) & (c == 2) & (m == 2))
            def _():
                lower_plane(1)

            key = s * 32 + c * 8 + m
            code = jnp.int32(0)
            for ss in range(2):
                for cc in range(4):
                    for mm, chunks in enumerate(GROUPS[ss][cc]):
                        here = key == ss * 32 + cc * 8 + mm
                        packed = sum((4 * e + g) << (4 * q) for q, (e, g) in enumerate(chunks))
                        code = jnp.where(here, packed, code)

                        @pl.when(here)
                        def _(ss=ss, cc=cc, mm=mm, chunks=chunks):
                            known = AHEAD.get((ss, cc, mm - 1), [])
                            for e, g in chunks + AHEAD.get((ss, cc, mm), []):
                                r = e // 2
                                if e % 2 == cc % 2 and (e, g) not in known:
                                    drain(rows_of(0, 0, (4 if g else 3) * PIECE), pr.at[ss, r, g])
                                    if r <= cc // 2 - cc % 2:
                                        ref = grid.at[ss, e, pl.ds(g * CHUNK, CHUNK), :]
                                        rdma(ref, ref, cs.at[ss, r], cr.at[ss, r, g], mate).start()
                            for e, g in chunks:
                                if e % 2 != cc % 2:
                                    drain(rows_of(0, 0, CHUNK), cr.at[ss, e // 2, g])

            blocks = [((code >> (4 * q + 2)) & 3, (code >> (4 * q)) & 3) for q in range(4)]

            short = (c == 0) | ((s == 1) & (((c == 2) & (m > 1)) | ((c == 3) & (m > 2))))

            @pl.when(short)
            def _():
                attend(blocks[:2])

            @pl.when(jnp.logical_not(short))
            def _():
                attend(blocks)

            return carry

        groups = jnp.maximum(c + 1, 2) + jnp.where((s == 1) & upper, 1, 0)
        lax.fori_loop(0, groups, group, 0)

        @pl.when((s == 0) & (c == 3))
        def _():
            lower_plane(1)

        @pl.when(s == 0)
        def _():
            loads[2].wait()
            loads[3].wait()

        sums = acc[...]
        flat[...] = (sums / sums[CHANS + 3 : CHANS + 4, :]).T
        attended = []
        for h in range(HEADS):
            zed = flat[pl.ds(h, ROWS, stride=HEADS), :]
            zed_hi = zed.astype(BF)
            zed_lo = (zed - zed_hi.astype(F32)).astype(BF)
            both = dot_nn(jnp.concatenate([zed_hi, zed_lo], axis=0), wv[:, h * HD : (h + 1) * HD])
            attended.append((both[0:ROWS] + both[ROWS:]).astype(BF))
        velocity = dot_nt(jnp.concatenate(attended, axis=1), wo[...])
        change = sigma(c, s + 1) - sigma(c, s)
        state[:, 0:CHANS] = state[:, 0:CHANS] + change[:, 0:CHANS] * velocity
        out_ref[1] = velocity
        return carry

    lax.fori_loop(0, 2, step, 0)
    out_ref[0] = state[:, 0:CHANS]

    def finish(s, carry):
        @pl.when(upper)
        def _():
            drain(grid.at[0, 0, pl.ds(0, 3 * ROWS), :], zs.at[s])

        @pl.when(jnp.logical_not(upper))
        def _():
            drain(grid.at[0, 0, pl.ds(0, 7 * ROWS), :], zs.at[s])

        def rail(r, carry):
            for g in range(4):
                drain(grid.at[0, 0, pl.ds(0, (4 if g else 3) * PIECE), :], ps.at[s, r, g])

            @pl.when(r <= zhi - core)
            def _():
                drain(grid.at[0, 0], cs.at[s, r])

            return carry

        lax.fori_loop(0, zhi + 1, rail, 0)
        return carry

    lax.fori_loop(0, 2, finish, 0)


def local(latent, step_index, w_query, w_key, w_value, cond, qk_gain, w_out):
    vmem = pl.BlockSpec(memory_space=pltpu.VMEM)
    smem = pl.BlockSpec(memory_space=pltpu.SMEM)
    hbm = pl.BlockSpec(memory_space=pl.ANY)
    dma = pltpu.SemaphoreType.DMA
    both = pl.pallas_call(
        kernel,
        out_shape=jax.ShapeDtypeStruct((2, ROWS, CHANS), F32),
        in_specs=[smem, smem, hbm, hbm, hbm, hbm, hbm, hbm],
        out_specs=vmem,
        scratch_shapes=[
            pltpu.VMEM((2, 4, SEQ, 128), BF),
            pltpu.VMEM((ROWS, CHANS), F32),
            pltpu.VMEM((3, WIDTH), F32),
            pltpu.VMEM((128, WIDTH), BF),
            pltpu.VMEM((128, WIDTH), BF),
            pltpu.VMEM((128, WIDTH), BF),
            pltpu.VMEM((CHANS, WIDTH), BF),
            pltpu.VMEM((4, 8, 128), F32),
            pltpu.VMEM((ROWS, 128), F32),
            pltpu.VMEM((QUERIES, 128), BF),
            pltpu.VMEM((QUERIES, 128), F32),
            pltpu.VMEM((128, QUERIES), F32),
            pltpu.VMEM((8, QUERIES), F32),
            dma((6,)),
            dma((2,)),
            dma((2, 2)),
            dma((2, 2, 4)),
            dma((2, 2, 4)),
            dma((2, 2)),
            dma((2, 2, 4)),
        ],
        compiler_params=pltpu.CompilerParams(
            collective_id=0, has_side_effects=True, vmem_limit_bytes=63 * 1024 * 1024
        ),
    )(step_index, qk_gain, latent[0], cond, w_query, w_key, w_value, w_out.T)
    return both[0:1], both[1:2]


def solution(mesh):
    return jax.shard_map(
        local,
        mesh=mesh,
        in_specs=(P("span", "tok", None), P(), P(), P(), P(), P(), P(), P()),
        out_specs=(P("span", "tok", None), P("span", "tok", None)),
        check_vma=False,
    )
```

```python
import jax
import jax.numpy as jnp
from jax import lax
from jax.experimental import pallas as pl
from jax.experimental.pallas import tpu as pltpu
from jax.sharding import PartitionSpec as P

MESH = pl.DeviceIdType.MESH
NSTEPS = 8
ROWS = 32
PIECE = 4 * ROWS
CHANS = 64
HEADS = 32
HD = 128
WIDTH = HEADS * HD
SEQ = 2048
CHUNK = SEQ // 4
QUERIES = HEADS * ROWS
COLS = QUERIES // 4
SUB = 64
LAG = 3
PLACES = (
    (0, 0), (1, 0), (3, 0), (0, 1), (0, 3), (1, 1), (3, 3), (1, 3),
    (3, 1), (2, 0), (0, 2), (2, 1), (2, 3), (1, 2), (3, 2), (2, 2),
)
WHOLE = [[(e, g) for g in range(4)] for e in range(4)]
GROUPS = (
    (
        [[(0, 0), (0, 1)], [(0, 2), (0, 3)]],
        [[(1, 0), (1, 1), (0, 0), (0, 1)], [(1, 2), (1, 3), (0, 2), (0, 3)]],
        [[(2, 0), (0, 0), (2, 1), (0, 1)], [(2, 2), (0, 2), (1, 0), (1, 1)], [(2, 3), (0, 3), (1, 2), (1, 3)]],
        [
            [(3, 0), (1, 0), (3, 1), (1, 1)],
            [(2, 0), (0, 0), (2, 1), (0, 1)],
            [(3, 2), (1, 2), (3, 3), (1, 3)],
            [(2, 2), (0, 2), (2, 3), (0, 3)],
        ],
    ),
    (
        [[(0, 0), (0, 1)], [(0, 2), (0, 3)]],
        [WHOLE[0], WHOLE[1]],
        [WHOLE[0], WHOLE[1], [(2, 0), (2, 1)], [(2, 2), (2, 3)]],
        [WHOLE[1], WHOLE[0], [(3, 0), (3, 1), (2, 0), (2, 1)], [(3, 2), (3, 3)], [(2, 2), (2, 3)]],
    ),
)
AHEAD = {(1, 2, 1): [(2, 0), (2, 1)], (1, 2, 2): [(2, 2), (2, 3)]}
LOG2E = 1.4426950408889634
BF = jnp.bfloat16
F32 = jnp.float32


def dot_nt(a, b):
    return lax.dot_general(a, b, (((1,), (1,)), ((), ())), preferred_element_type=F32)


def dot_nn(a, b):
    return jnp.dot(a, b, preferred_element_type=F32)


def kernel(
    step_ref, gain_ref, latent_hbm, cond_hbm, wq_hbm, wk_hbm, wv_hbm, wo_hbm,
    out_ref,
    grid, latent_ref, cond_ref, wq, wk, wv, wo, aug, state, q2, flat, acc, top,
    wsem, zs, zr, ps, pr, cs, cr,
):
    c = lax.axis_index("span")
    t = lax.axis_index("tok")
    zhi = c >> 1
    core = c & 1
    y = t >> 4
    zl = (t >> 2) & 3
    x = t & 3
    upper = zhi == 1

    def tok(yy, zz, xx):
        return (yy << 4) | (zz << 2) | xx

    def plane_peer(place):
        return c, tok((y + place[0]) & 3, zl, (x + place[1]) & 3)

    across_z = (1 - zhi) * 2 + core
    mate = (zhi * 2 + 1 - core, t)

    barrier = pltpu.get_barrier_semaphore()

    def greet(dev):
        pl.semaphore_signal(barrier, inc=1, device_id=dev, device_id_type=MESH)

    for d in range(1, 4):
        greet((c, tok(y, (zl + d) & 3, x)))
    for d in range(4):
        greet((across_z, tok(y, d, x)))
    for place in PLACES[1:]:
        greet(plane_peer(place))
    greet(mate)

    loads = [
        pltpu.make_async_copy(wk_hbm, wk.at[pl.ds(0, CHANS), :], wsem.at[0]),
        pltpu.make_async_copy(wq_hbm, wq.at[pl.ds(0, CHANS), :], wsem.at[1]),
        pltpu.make_async_copy(wv_hbm, wv.at[pl.ds(0, CHANS), :], wsem.at[2]),
        pltpu.make_async_copy(wo_hbm, wo, wsem.at[3]),
        pltpu.make_async_copy(cond_hbm, cond_ref, wsem.at[4]),
        pltpu.make_async_copy(latent_hbm, latent_ref, wsem.at[5]),
    ]
    for n in (4, 0, 5, 1, 2, 3):
        loads[n].start()

    lane = lax.broadcasted_iota(jnp.int32, (1, 128), 1)
    loads[4].wait()
    row16 = lax.broadcasted_iota(jnp.int32, (16, WIDTH), 0)
    for which, ref in enumerate((wq, wk, wv)):
        cvec = cond_ref[which : which + 1, :]
        chi = cvec.astype(BF).astype(F32)
        clo = cvec - chi
        rows = jnp.where((row16 == 0) | (row16 == 2), chi, jnp.where(row16 == 1, clo, 0.0))
        ref[CHANS : CHANS + 16, :] = rows.astype(BF)
        ref[CHANS + 16 :, :] = jnp.zeros((128 - CHANS - 16, WIDTH), BF)
    gk = jnp.zeros((1, 128), F32)
    for h in range(HEADS):
        gk = jnp.where((lane == CHANS + h) | (lane == CHANS + HEADS + h), gain_ref[1, h], gk)
    gk = gk * (HD ** (-0.5) * LOG2E)
    down = lax.broadcasted_iota(jnp.int32, (128, 128), 0)
    across = lax.broadcasted_iota(jnp.int32, (128, 128), 1)
    spread = jnp.where((down >= CHANS) & (down % HEADS == across % HEADS), 1.0, 0.0).astype(BF)
    eye = jnp.where(down == across, 1.0, 0.0).astype(BF)
    pmask = jnp.where(lane < CHANS, 1.0, 0.0)
    state[...] = jnp.zeros_like(state)
    loads[5].wait()
    state[:, 0:CHANS] = latent_ref[...]

    def sigma(span, extra):
        level = jnp.full((1, 128), step_ref[span] + extra, jnp.int32).astype(F32)
        frac = 1.0 - level / NSTEPS
        return 3.0 * frac / (1.0 + 2.0 * frac)

    def rdma(src, dst, send, recv, dev):
        return pltpu.make_async_remote_copy(
            src_ref=src, dst_ref=dst, send_sem=send, recv_sem=recv, device_id=dev, device_id_type=MESH
        )

    def drain(ref, sem):
        pltpu.make_async_copy(ref, ref, sem).wait()

    loads[0].wait()

    def step(s, carry):
        def rows_of(e, at, count):
            return grid.at[s, e, pl.ds(at, count), :]

        def chunk_of(e, g):
            at = pl.multiple_of(g * CHUNK, CHUNK)
            return grid.at[s, e, pl.ds(at, CHUNK), :]

        for span in range(4):
            sig = sigma(span, s)
            shi = sig.astype(BF).astype(F32)
            slo = sig - shi
            line = jnp.where(
                (lane == CHANS) | (lane == CHANS + 1) | (lane == CHANS + 4),
                shi,
                jnp.where(lane == CHANS + 2, slo, jnp.where(lane == CHANS + 3, 1.0, 0.0)),
            )
            aug[span] = jnp.broadcast_to(line, (8, 128))
        patches = state[...]
        own = (patches + aug[c][0:1, :]).astype(BF)

        squares = jnp.zeros((ROWS, 128), F32)
        pk = dot_nn(own, wk[...])
        for h in range(HEADS):
            part = pk[:, h * HD : (h + 1) * HD]
            ms = jnp.sum(part * part, axis=-1, keepdims=True)
            squares = jnp.where((lane == CHANS + h) | (lane == CHANS + HEADS + h), ms, squares)
        factor = gk / jnp.sqrt(squares * (1.0 / HD) + 1e-06)
        fhi = factor.astype(BF).astype(F32)
        row = jnp.where(lane < CHANS, patches, jnp.where(lane < CHANS + HEADS, fhi, factor - fhi)).astype(BF)
        at = pl.multiple_of(zl * ROWS, ROWS)
        grid[s, c, pl.ds(at, ROWS), :] = row

        @pl.when(s == 0)
        def _():
            pl.semaphore_wait(barrier, 23)

        block = rows_of(c, at, ROWS)
        @pl.when(jnp.logical_not(upper))
        def _():
            for d in range(4):
                rdma(block, block, zs.at[s], zr.at[s, 0], (across_z, tok(y, d, x))).start()

        for d in range(1, 4):
            rdma(block, block, zs.at[s], zr.at[s, zhi], (c, tok(y, (zl + d) & 3, x))).start()

        def send_chunk(ss, r, g):
            e = core + 2 * r
            for slot in range(max(4 * g, 1), 4 * g + 4):
                rdma(
                    grid.at[ss, e, pl.ds(0, PIECE), :],
                    grid.at[ss, e, pl.ds(slot * PIECE, PIECE), :],
                    ps.at[ss, r, g],
                    pr.at[ss, r, g],
                    plane_peer((-PLACES[slot][0], -PLACES[slot][1])),
                ).start()

        def own_plane():
            drain(rows_of(0, 0, 3 * ROWS), zr.at[s, zhi])
            for g in range(4):
                send_chunk(s, zhi, g)

        def lower_plane(ss):
            drain(rows_of(0, 0, 4 * ROWS), zr.at[ss, 0])
            for g in range(4):
                send_chunk(ss, 0, g)

        @pl.when(s == 0)
        def _():
            loads[1].wait()

        pq = dot_nn(own, wq[...])
        normed = []
        for h in range(HEADS):
            part = pq[:, h * HD : (h + 1) * HD]
            ms = jnp.sum(part * part, axis=-1, keepdims=True) * (1.0 / HD)
            normed.append((part / jnp.sqrt(ms + 1e-06) * gain_ref[0, h]).astype(BF))
        for h in range(HEADS):
            flat[pl.ds(h, ROWS, stride=HEADS), :] = dot_nt(normed[h], wk[:, h * HD : (h + 1) * HD])
        qk = flat[...]
        rest = pltpu.roll(qk - qk.astype(BF).astype(F32), 4, 1)
        q2[...] = jnp.where(lane == CHANS + 4, rest, qk).astype(BF)
        acc[...] = jnp.zeros_like(acc)
        top[...] = jnp.full_like(top, -1e30)
        @pl.when(jnp.logical_not(upper) | (s == 1))
        def _():
            own_plane()

        @pl.when(upper & (s == 0))
        def _():
            drain(rows_of(0, 0, 3 * ROWS), zr.at[s, 1])
            for g in range(2):
                send_chunk(s, 1, g)
            drain(rows_of(0, 0, 4 * ROWS), zr.at[s, 0])
            for g in range(2):
                send_chunk(s, 0, g)
            for g in range(2, 4):
                for r in range(2):
                    send_chunk(s, r, g)

        def attend(blocks):
            keys, factors, turned = [], [], []
            for e, g in blocks:
                rows = chunk_of(e, g)[...]
                plain = rows * pmask.astype(BF) + aug[e][0:1, :].astype(BF)
                keys.append(plain)
                factors.append(dot_nn(rows, spread))
                turned.append(dot_nt(eye, plain).astype(BF))
            units = [(b, slice(u * COLS, (u + 1) * COLS)) for b in range(len(blocks)) for u in range(QUERIES // COLS)]

            def score(n):
                b, cols = units[n]
                return dot_nt(keys[b], q2[cols, :])

            def soften(n, raw):
                b, cols = units[n]
                scaled, best = [], None
                for at in range(0, CHUNK, SUB):
                    wide = jnp.concatenate([factors[b][at : at + SUB, :]] * (COLS // 128), axis=1)
                    part = raw[at : at + SUB, :] * wide
                    scaled.append(part)
                    high = jnp.max(part.reshape(SUB // 8, 8, COLS), axis=0)
                    best = high if best is None else jnp.maximum(best, high)
                old = top[0:1, cols]
                new = jnp.maximum(old, jnp.max(best, axis=0, keepdims=True))
                top[0:1, cols] = new
                weights = [jnp.exp2(part - new).astype(BF) for part in scaled]
                return n, jnp.concatenate(weights, axis=0), jnp.exp2(old - new)

            def gather(n, weights, alpha):
                b, cols = units[n]
                acc[:, cols] = acc[:, cols] * alpha + dot_nn(turned[b], weights)

            raw = score(0)
            pending = []
            for n in range(len(units)):
                later = score(n + 1) if n + 1 < len(units) else None
                pending.append(soften(n, raw))
                raw = later
                if len(pending) > LAG:
                    gather(*pending.pop(0))
            for item in pending:
                gather(*item)

        def group(m, carry):
            @pl.when((s == 0) & (c == 2) & (m == 2))
            def _():
                lower_plane(1)

            key = s * 32 + c * 8 + m
            code = jnp.int32(0)
            for ss in range(2):
                for cc in range(4):
                    for mm, chunks in enumerate(GROUPS[ss][cc]):
                        here = key == ss * 32 + cc * 8 + mm
                        packed = sum((4 * e + g) << (4 * q) for q, (e, g) in enumerate(chunks))
                        code = jnp.where(here, packed, code)

                        @pl.when(here)
                        def _(ss=ss, cc=cc, mm=mm, chunks=chunks):
                            known = AHEAD.get((ss, cc, mm - 1), [])
                            for e, g in chunks + AHEAD.get((ss, cc, mm), []):
                                r = e // 2
                                if e % 2 == cc % 2 and (e, g) not in known:
                                    drain(rows_of(0, 0, (4 if g else 3) * PIECE), pr.at[ss, r, g])
                                    if r <= cc // 2 - cc % 2:
                                        ref = grid.at[ss, e, pl.ds(g * CHUNK, CHUNK), :]
                                        rdma(ref, ref, cs.at[ss, r], cr.at[ss, r, g], mate).start()
                            for e, g in chunks:
                                if e % 2 != cc % 2:
                                    drain(rows_of(0, 0, CHUNK), cr.at[ss, e // 2, g])

            blocks = [((code >> (4 * q + 2)) & 3, (code >> (4 * q)) & 3) for q in range(4)]

            short = (c == 0) | ((s == 1) & (((c == 2) & (m > 1)) | ((c == 3) & (m > 2))))

            @pl.when(short)
            def _():
                attend(blocks[:2])

            @pl.when(jnp.logical_not(short))
            def _():
                attend(blocks)

            return carry

        groups = jnp.maximum(c + 1, 2) + jnp.where((s == 1) & upper, 1, 0)
        lax.fori_loop(0, groups, group, 0)

        @pl.when((s == 0) & (c == 3))
        def _():
            lower_plane(1)

        @pl.when(s == 0)
        def _():
            loads[2].wait()
            loads[3].wait()

        sums = acc[...]
        flat[...] = (sums / sums[CHANS + 3 : CHANS + 4, :]).T
        attended = []
        for h in range(HEADS):
            zed = flat[pl.ds(h, ROWS, stride=HEADS), :]
            zed_hi = zed.astype(BF)
            zed_lo = (zed - zed_hi.astype(F32)).astype(BF)
            both = dot_nn(jnp.concatenate([zed_hi, zed_lo], axis=0), wv[:, h * HD : (h + 1) * HD])
            attended.append((both[0:ROWS] + both[ROWS:]).astype(BF))
        velocity = dot_nt(jnp.concatenate(attended, axis=1), wo[...])
        change = sigma(c, s + 1) - sigma(c, s)
        state[:, 0:CHANS] = state[:, 0:CHANS] + change[:, 0:CHANS] * velocity
        out_ref[1] = velocity
        return carry

    lax.fori_loop(0, 2, step, 0)
    out_ref[0] = state[:, 0:CHANS]

    def finish(s, carry):
        @pl.when(upper)
        def _():
            drain(grid.at[0, 0, pl.ds(0, 3 * ROWS), :], zs.at[s])

        @pl.when(jnp.logical_not(upper))
        def _():
            drain(grid.at[0, 0, pl.ds(0, 7 * ROWS), :], zs.at[s])

        def rail(r, carry):
            for g in range(4):
                drain(grid.at[0, 0, pl.ds(0, (4 if g else 3) * PIECE), :], ps.at[s, r, g])

            @pl.when(r <= zhi - core)
            def _():
                drain(grid.at[0, 0], cs.at[s, r])

            return carry

        lax.fori_loop(0, zhi + 1, rail, 0)
        return carry

    lax.fori_loop(0, 2, finish, 0)


def local(latent, step_index, w_query, w_key, w_value, cond, qk_gain, w_out):
    vmem = pl.BlockSpec(memory_space=pltpu.VMEM)
    smem = pl.BlockSpec(memory_space=pltpu.SMEM)
    hbm = pl.BlockSpec(memory_space=pl.ANY)
    dma = pltpu.SemaphoreType.DMA
    both = pl.pallas_call(
        kernel,
        out_shape=jax.ShapeDtypeStruct((2, ROWS, CHANS), F32),
        in_specs=[smem, smem, hbm, hbm, hbm, hbm, hbm, hbm],
        out_specs=vmem,
        scratch_shapes=[
            pltpu.VMEM((2, 4, SEQ, 128), BF),
            pltpu.VMEM((ROWS, CHANS), F32),
            pltpu.VMEM((3, WIDTH), F32),
            pltpu.VMEM((128, WIDTH), BF),
            pltpu.VMEM((128, WIDTH), BF),
            pltpu.VMEM((128, WIDTH), BF),
            pltpu.VMEM((CHANS, WIDTH), BF),
            pltpu.VMEM((4, 8, 128), F32),
            pltpu.VMEM((ROWS, 128), F32),
            pltpu.VMEM((QUERIES, 128), BF),
            pltpu.VMEM((QUERIES, 128), F32),
            pltpu.VMEM((128, QUERIES), F32),
            pltpu.VMEM((8, QUERIES), F32),
            dma((6,)),
            dma((2,)),
            dma((2, 2)),
            dma((2, 2, 4)),
            dma((2, 2, 4)),
            dma((2, 2)),
            dma((2, 2, 4)),
        ],
        compiler_params=pltpu.CompilerParams(
            collective_id=0, has_side_effects=True, vmem_limit_bytes=63 * 1024 * 1024
        ),
    )(step_index, qk_gain, latent[0], cond, w_query, w_key, w_value, w_out.T)
    return both[0:1], both[1:2]


def solution(mesh):
    return jax.shard_map(
        local,
        mesh=mesh,
        in_specs=(P("span", "tok", None), P(), P(), P(), P(), P(), P(), P()),
        out_specs=(P("span", "tok", None), P("span", "tok", None)),
        check_vma=False,
    )
```

```python
import jax
import jax.numpy as jnp
from jax import lax
from jax.experimental import pallas as pl
from jax.experimental.pallas import tpu as pltpu
from jax.sharding import PartitionSpec as P

MESH = pl.DeviceIdType.MESH
NSTEPS = 8
ROWS = 32
PIECE = 4 * ROWS
CHANS = 64
HEADS = 32
HD = 128
WIDTH = HEADS * HD
SEQ = 2048
CHUNK = SEQ // 4
QUERIES = HEADS * ROWS
COLS = QUERIES // 4
SUB = 64
LAG = 3
PLACES = (
    (0, 0), (1, 0), (3, 0), (0, 1), (0, 3), (1, 1), (3, 3), (1, 3),
    (3, 1), (2, 0), (0, 2), (2, 1), (2, 3), (1, 2), (3, 2), (2, 2),
)
WHOLE = [[(e, g) for g in range(4)] for e in range(4)]
GROUPS = (
    (
        [[(0, 0), (0, 1)], [(0, 2), (0, 3)]],
        [[(1, 0), (1, 1), (0, 0), (0, 1)], [(1, 2), (1, 3), (0, 2), (0, 3)]],
        [[(2, 0), (0, 0), (2, 1), (0, 1)], [(2, 2), (0, 2), (1, 0), (1, 1)], [(2, 3), (0, 3), (1, 2), (1, 3)]],
        [
            [(3, 0), (1, 0), (3, 1), (1, 1)],
            [(2, 0), (0, 0), (2, 1), (0, 1)],
            [(3, 2), (1, 2), (3, 3), (1, 3)],
            [(2, 2), (0, 2), (2, 3), (0, 3)],
        ],
    ),
    (
        [[(0, 0), (0, 1)], [(0, 2), (0, 3)]],
        [WHOLE[0], WHOLE[1]],
        [WHOLE[0], WHOLE[1], [(2, 0), (2, 1)], [(2, 2), (2, 3)]],
        [WHOLE[0], WHOLE[1], [(3, 0), (3, 1), (2, 0), (2, 1)], [(3, 2), (3, 3)], [(2, 2), (2, 3)]],
    ),
)
AHEAD = {(1, 2, 1): [(2, 0), (2, 1)], (1, 2, 2): [(2, 2), (2, 3)]}
LOG2E = 1.4426950408889634
BF = jnp.bfloat16
F32 = jnp.float32


def dot_nt(a, b):
    return lax.dot_general(a, b, (((1,), (1,)), ((), ())), preferred_element_type=F32)


def dot_nn(a, b):
    return jnp.dot(a, b, preferred_element_type=F32)


def kernel(
    step_ref, gain_ref, latent_hbm, cond_hbm, wq_hbm, wk_hbm, wv_hbm, wo_hbm,
    out_ref,
    grid, latent_ref, cond_ref, wq, wk, wv, wo, aug, state, q2, flat, acc, top,
    wsem, zs, zr, ps, pr, cs, cr,
):
    c = lax.axis_index("span")
    t = lax.axis_index("tok")
    zhi = c >> 1
    core = c & 1
    y = t >> 4
    zl = (t >> 2) & 3
    x = t & 3
    upper = zhi == 1

    def tok(yy, zz, xx):
        return (yy << 4) | (zz << 2) | xx

    def plane_peer(place):
        return c, tok((y + place[0]) & 3, zl, (x + place[1]) & 3)

    across_z = (1 - zhi) * 2 + core
    mate = (zhi * 2 + 1 - core, t)

    barrier = pltpu.get_barrier_semaphore()

    def greet(dev):
        pl.semaphore_signal(barrier, inc=1, device_id=dev, device_id_type=MESH)

    for d in range(1, 4):
        greet((c, tok(y, (zl + d) & 3, x)))
    for d in range(4):
        greet((across_z, tok(y, d, x)))
    for place in PLACES[1:]:
        greet(plane_peer(place))
    greet(mate)

    loads = [
        pltpu.make_async_copy(wk_hbm, wk.at[pl.ds(0, CHANS), :], wsem.at[0]),
        pltpu.make_async_copy(wq_hbm, wq.at[pl.ds(0, CHANS), :], wsem.at[1]),
        pltpu.make_async_copy(wv_hbm, wv.at[pl.ds(0, CHANS), :], wsem.at[2]),
        pltpu.make_async_copy(wo_hbm, wo, wsem.at[3]),
        pltpu.make_async_copy(cond_hbm, cond_ref, wsem.at[4]),
        pltpu.make_async_copy(latent_hbm, latent_ref, wsem.at[5]),
    ]
    for n in (4, 0, 5, 1, 2, 3):
        loads[n].start()

    lane = lax.broadcasted_iota(jnp.int32, (1, 128), 1)
    loads[4].wait()
    row16 = lax.broadcasted_iota(jnp.int32, (16, WIDTH), 0)
    for which, ref in enumerate((wq, wk, wv)):
        cvec = cond_ref[which : which + 1, :]
        chi = cvec.astype(BF).astype(F32)
        clo = cvec - chi
        rows = jnp.where((row16 == 0) | (row16 == 2), chi, jnp.where(row16 == 1, clo, 0.0))
        ref[CHANS : CHANS + 16, :] = rows.astype(BF)
        ref[CHANS + 16 :, :] = jnp.zeros((128 - CHANS - 16, WIDTH), BF)
    gk = jnp.zeros((1, 128), F32)
    for h in range(HEADS):
        gk = jnp.where((lane == CHANS + h) | (lane == CHANS + HEADS + h), gain_ref[1, h], gk)
    gk = gk * (HD ** (-0.5) * LOG2E)
    down = lax.broadcasted_iota(jnp.int32, (128, 128), 0)
    across = lax.broadcasted_iota(jnp.int32, (128, 128), 1)
    spread = jnp.where((down >= CHANS) & (down % HEADS == across % HEADS), 1.0, 0.0).astype(BF)
    eye = jnp.where(down == across, 1.0, 0.0).astype(BF)
    pmask = jnp.where(lane < CHANS, 1.0, 0.0)
    state[...] = jnp.zeros_like(state)
    loads[5].wait()
    state[:, 0:CHANS] = latent_ref[...]

    def sigma(span, extra):
        level = jnp.full((1, 128), step_ref[span] + extra, jnp.int32).astype(F32)
        frac = 1.0 - level / NSTEPS
        return 3.0 * frac / (1.0 + 2.0 * frac)

    def rdma(src, dst, send, recv, dev):
        return pltpu.make_async_remote_copy(
            src_ref=src, dst_ref=dst, send_sem=send, recv_sem=recv, device_id=dev, device_id_type=MESH
        )

    def drain(ref, sem):
        pltpu.make_async_copy(ref, ref, sem).wait()

    loads[0].wait()

    def step(s, carry):
        def rows_of(e, at, count):
            return grid.at[s, e, pl.ds(at, count), :]

        def chunk_of(e, g):
            at = pl.multiple_of(g * CHUNK, CHUNK)
            return grid.at[s, e, pl.ds(at, CHUNK), :]

        for span in range(4):
            sig = sigma(span, s)
            shi = sig.astype(BF).astype(F32)
            slo = sig - shi
            line = jnp.where(
                (lane == CHANS) | (lane == CHANS + 1) | (lane == CHANS + 4),
                shi,
                jnp.where(lane == CHANS + 2, slo, jnp.where(lane == CHANS + 3, 1.0, 0.0)),
            )
            aug[span] = jnp.broadcast_to(line, (8, 128))
        patches = state[...]
        own = (patches + aug[c][0:1, :]).astype(BF)

        squares = jnp.zeros((ROWS, 128), F32)
        pk = dot_nn(own, wk[...])
        for h in range(HEADS):
            part = pk[:, h * HD : (h + 1) * HD]
            ms = jnp.sum(part * part, axis=-1, keepdims=True)
            squares = jnp.where((lane == CHANS + h) | (lane == CHANS + HEADS + h), ms, squares)
        factor = gk / jnp.sqrt(squares * (1.0 / HD) + 1e-06)
        fhi = factor.astype(BF).astype(F32)
        row = jnp.where(lane < CHANS, patches, jnp.where(lane < CHANS + HEADS, fhi, factor - fhi)).astype(BF)
        at = pl.multiple_of(zl * ROWS, ROWS)
        grid[s, c, pl.ds(at, ROWS), :] = row

        @pl.when(s == 0)
        def _():
            pl.semaphore_wait(barrier, 23)

        block = rows_of(c, at, ROWS)
        @pl.when(jnp.logical_not(upper))
        def _():
            for d in range(4):
                rdma(block, block, zs.at[s], zr.at[s, 0], (across_z, tok(y, d, x))).start()

        for d in range(1, 4):
            rdma(block, block, zs.at[s], zr.at[s, zhi], (c, tok(y, (zl + d) & 3, x))).start()

        def send_chunk(ss, r, g):
            e = core + 2 * r
            for slot in range(max(4 * g, 1), 4 * g + 4):
                rdma(
                    grid.at[ss, e, pl.ds(0, PIECE), :],
                    grid.at[ss, e, pl.ds(slot * PIECE, PIECE), :],
                    ps.at[ss, r, g],
                    pr.at[ss, r, g],
                    plane_peer((-PLACES[slot][0], -PLACES[slot][1])),
                ).start()

        def own_plane():
            drain(rows_of(0, 0, 3 * ROWS), zr.at[s, zhi])
            for g in range(4):
                send_chunk(s, zhi, g)

        def lower_plane(ss):
            drain(rows_of(0, 0, 4 * ROWS), zr.at[ss, 0])
            for g in range(4):
                send_chunk(ss, 0, g)

        @pl.when(s == 0)
        def _():
            loads[1].wait()

        pq = dot_nn(own, wq[...])
        normed = []
        for h in range(HEADS):
            part = pq[:, h * HD : (h + 1) * HD]
            ms = jnp.sum(part * part, axis=-1, keepdims=True) * (1.0 / HD)
            normed.append((part / jnp.sqrt(ms + 1e-06) * gain_ref[0, h]).astype(BF))
        for h in range(HEADS):
            flat[pl.ds(h, ROWS, stride=HEADS), :] = dot_nt(normed[h], wk[:, h * HD : (h + 1) * HD])
        qk = flat[...]
        rest = pltpu.roll(qk - qk.astype(BF).astype(F32), 4, 1)
        q2[...] = jnp.where(lane == CHANS + 4, rest, qk).astype(BF)
        acc[...] = jnp.zeros_like(acc)
        top[...] = jnp.full_like(top, -1e30)
        @pl.when(jnp.logical_not(upper) | (s == 1))
        def _():
            own_plane()

        @pl.when(upper & (s == 0))
        def _():
            drain(rows_of(0, 0, 3 * ROWS), zr.at[s, 1])
            for g in range(2):
                send_chunk(s, 1, g)
            drain(rows_of(0, 0, 4 * ROWS), zr.at[s, 0])
            for g in range(2):
                send_chunk(s, 0, g)
            for g in range(2, 4):
                for r in range(2):
                    send_chunk(s, r, g)

        def attend(blocks):
            keys, factors, turned = [], [], []
            for e, g in blocks:
                rows = chunk_of(e, g)[...]
                plain = rows * pmask.astype(BF) + aug[e][0:1, :].astype(BF)
                keys.append(plain)
                factors.append(dot_nn(rows, spread))
                turned.append(dot_nt(eye, plain).astype(BF))
            units = [(b, slice(u * COLS, (u + 1) * COLS)) for b in range(len(blocks)) for u in range(QUERIES // COLS)]

            def score(n):
                b, cols = units[n]
                return dot_nt(keys[b], q2[cols, :])

            def soften(n, raw):
                b, cols = units[n]
                scaled, best = [], None
                for at in range(0, CHUNK, SUB):
                    wide = jnp.concatenate([factors[b][at : at + SUB, :]] * (COLS // 128), axis=1)
                    part = raw[at : at + SUB, :] * wide
                    scaled.append(part)
                    high = jnp.max(part.reshape(SUB // 8, 8, COLS), axis=0)
                    best = high if best is None else jnp.maximum(best, high)
                old = top[0:1, cols]
                new = jnp.maximum(old, jnp.max(best, axis=0, keepdims=True))
                top[0:1, cols] = new
                weights = [jnp.exp2(part - new).astype(BF) for part in scaled]
                return n, jnp.concatenate(weights, axis=0), jnp.exp2(old - new)

            def gather(n, weights, alpha):
                b, cols = units[n]
                acc[:, cols] = acc[:, cols] * alpha + dot_nn(turned[b], weights)

            raw = score(0)
            pending = []
            for n in range(len(units)):
                later = score(n + 1) if n + 1 < len(units) else None
                pending.append(soften(n, raw))
                raw = later
                if len(pending) > LAG:
                    gather(*pending.pop(0))
            for item in pending:
                gather(*item)

        def group(m, carry):
            @pl.when((s == 0) & (c == 2) & (m == 2))
            def _():
                lower_plane(1)

            key = s * 32 + c * 8 + m
            code = jnp.int32(0)
            for ss in range(2):
                for cc in range(4):
                    for mm, chunks in enumerate(GROUPS[ss][cc]):
                        here = key == ss * 32 + cc * 8 + mm
                        packed = sum((4 * e + g) << (4 * q) for q, (e, g) in enumerate(chunks))
                        code = jnp.where(here, packed, code)

                        @pl.when(here)
                        def _(ss=ss, cc=cc, mm=mm, chunks=chunks):
                            known = AHEAD.get((ss, cc, mm - 1), [])
                            for e, g in chunks + AHEAD.get((ss, cc, mm), []):
                                r = e // 2
                                if e % 2 == cc % 2 and (e, g) not in known:
                                    drain(rows_of(0, 0, (4 if g else 3) * PIECE), pr.at[ss, r, g])
                                    if r <= cc // 2 - cc % 2:
                                        ref = grid.at[ss, e, pl.ds(g * CHUNK, CHUNK), :]
                                        rdma(ref, ref, cs.at[ss, r], cr.at[ss, r, g], mate).start()
                            for e, g in chunks:
                                if e % 2 != cc % 2:
                                    drain(rows_of(0, 0, CHUNK), cr.at[ss, e // 2, g])

            blocks = [((code >> (4 * q + 2)) & 3, (code >> (4 * q)) & 3) for q in range(4)]

            short = (c == 0) | ((s == 1) & (((c == 2) & (m > 1)) | ((c == 3) & (m > 2))))

            @pl.when(short)
            def _():
                attend(blocks[:2])

            @pl.when(jnp.logical_not(short))
            def _():
                attend(blocks)

            return carry

        groups = jnp.maximum(c + 1, 2) + jnp.where((s == 1) & upper, 1, 0)
        lax.fori_loop(0, groups, group, 0)

        @pl.when((s == 0) & (c == 3))
        def _():
            lower_plane(1)

        @pl.when(s == 0)
        def _():
            loads[2].wait()
            loads[3].wait()

        sums = acc[...]
        flat[...] = (sums / sums[CHANS + 3 : CHANS + 4, :]).T
        attended = []
        for h in range(HEADS):
            zed = flat[pl.ds(h, ROWS, stride=HEADS), :]
            zed_hi = zed.astype(BF)
            zed_lo = (zed - zed_hi.astype(F32)).astype(BF)
            both = dot_nn(jnp.concatenate([zed_hi, zed_lo], axis=0), wv[:, h * HD : (h + 1) * HD])
            attended.append((both[0:ROWS] + both[ROWS:]).astype(BF))
        velocity = dot_nt(jnp.concatenate(attended, axis=1), wo[...])
        change = sigma(c, s + 1) - sigma(c, s)
        state[:, 0:CHANS] = state[:, 0:CHANS] + change[:, 0:CHANS] * velocity
        out_ref[1] = velocity
        return carry

    lax.fori_loop(0, 2, step, 0)
    out_ref[0] = state[:, 0:CHANS]

    def finish(s, carry):
        @pl.when(upper)
        def _():
            drain(grid.at[0, 0, pl.ds(0, 3 * ROWS), :], zs.at[s])

        @pl.when(jnp.logical_not(upper))
        def _():
            drain(grid.at[0, 0, pl.ds(0, 7 * ROWS), :], zs.at[s])

        def rail(r, carry):
            for g in range(4):
                drain(grid.at[0, 0, pl.ds(0, (4 if g else 3) * PIECE), :], ps.at[s, r, g])

            @pl.when(r <= zhi - core)
            def _():
                drain(grid.at[0, 0], cs.at[s, r])

            return carry

        lax.fori_loop(0, zhi + 1, rail, 0)
        return carry

    lax.fori_loop(0, 2, finish, 0)


def local(latent, step_index, w_query, w_key, w_value, cond, qk_gain, w_out):
    vmem = pl.BlockSpec(memory_space=pltpu.VMEM)
    smem = pl.BlockSpec(memory_space=pltpu.SMEM)
    hbm = pl.BlockSpec(memory_space=pl.ANY)
    dma = pltpu.SemaphoreType.DMA
    both = pl.pallas_call(
        kernel,
        out_shape=jax.ShapeDtypeStruct((2, ROWS, CHANS), F32),
        in_specs=[smem, smem, hbm, hbm, hbm, hbm, hbm, hbm],
        out_specs=vmem,
        scratch_shapes=[
            pltpu.VMEM((2, 4, SEQ, 128), BF),
            pltpu.VMEM((ROWS, CHANS), F32),
            pltpu.VMEM((3, WIDTH), F32),
            pltpu.VMEM((128, WIDTH), BF),
            pltpu.VMEM((128, WIDTH), BF),
            pltpu.VMEM((128, WIDTH), BF),
            pltpu.VMEM((CHANS, WIDTH), BF),
            pltpu.VMEM((4, 8, 128), F32),
            pltpu.VMEM((ROWS, 128), F32),
            pltpu.VMEM((QUERIES, 128), BF),
            pltpu.VMEM((QUERIES, 128), F32),
            pltpu.VMEM((128, QUERIES), F32),
            pltpu.VMEM((8, QUERIES), F32),
            dma((6,)),
            dma((2,)),
            dma((2, 2)),
            dma((2, 2, 4)),
            dma((2, 2, 4)),
            dma((2, 2)),
            dma((2, 2, 4)),
        ],
        compiler_params=pltpu.CompilerParams(
            collective_id=0, has_side_effects=True, vmem_limit_bytes=63 * 1024 * 1024
        ),
    )(step_index, qk_gain, latent[0], cond, w_query, w_key, w_value, w_out.T)
    return both[0:1], both[1:2]


def solution(mesh):
    return jax.shard_map(
        local,
        mesh=mesh,
        in_specs=(P("span", "tok", None), P(), P(), P(), P(), P(), P(), P()),
        out_specs=(P("span", "tok", None), P("span", "tok", None)),
        check_vma=False,
    )
```
